512 devices in a mesh: wave: 32 (over y, x), lev: 16 (over z, core).
Axes of the slice: x: 4, y: 8, z: 8, core: 2. Of those that a mesh axis runs over, the one named last changes fastest.
Arguments:
- spec: bfloat16 [2, 3, 16, 1280, 1280], P(None, None, 'lev', 'wave'), may hold values from -0.0048828125 to 0.0048828125
- legendre: bfloat16 [1280, 1280, 64], P('wave', 'lev'), may hold values from -4 to 4
- mids: int32 [1280], replicated, may hold values from 0 to 1279, each once
- band_lats: int32 [32], replicated, may hold values from 1 to 8, 128 in all
- nlon: int32 [64], replicated, may hold values from 1296 to 5136, as said below
Outputs:
- grid: bfloat16 [256, 3, 16, 5136], P('wave', None, 'lev')
The draws below stay inside these ranges and needn't reach their ends.
Inputs may be any that keep to these rules, and one draw needn't show every extreme that they name: `mids`: each wavenumber appears in exactly one slot; index i of wave holds slots i * 40 to (i + 1) * 40 - 1. `band_lats`: the bands sum to 128 latitudes. `nlon`: every entry is 4 i + 16 for a whole number i.
All inputs are finite; a program needn't handle non-finite values.
Results may differ from the reference program's by a relative error of at most 0.02.
Values may be sent and summed in bfloat16 or wider, within the bound.
A program may use at most 128 MiB of HBM per device.

```python
import math
import jax
import jax.numpy as jnp
import numpy as np
from jax import lax

TRUNC = 1279
FIELDS = 3
MW = 1280
LEVELS = 16
LAT_MAX = 8
LATS = 128
PAIRS = 64
NLON_MAX = 5136
KH = 41
N_WAVE = 32
N_LEV = 16


def draw_nlon(key, part):
    first_key, second_key = jax.random.split(key)
    cycles = jax.random.randint(first_key, (PAIRS,), (TRUNC + 1) // 4, TRUNC + 2)
    shuffled = jax.random.permutation(second_key, PAIRS)
    cycles = cycles.at[shuffled[0]].set(TRUNC + 1)
    cycles = cycles.at[shuffled[1]].set((TRUNC + 1) // 4)
    return (4 * cycles + 16).astype(jnp.int32)


def raised(array, stream_key, source, target, shards_of, factor):
    owner, partner = [(jnp.arange(array.shape[axis_at]) // (array.shape[axis_at] // shards_of)).reshape([-1 if axis == axis_at else 1 for axis in range(array.ndim)]) for axis_at in (source, target)]
    chosen = jax.random.permutation(stream_key, shards_of)[partner]
    strong = (owner == chosen) | (owner == (partner + shards_of // 2) % shards_of)
    return jnp.where(strong, factor * array, array)


def block_levels(own_key, dims, cuts, low, top_value):
    gain, own = 1.0, jax.random.fold_in(own_key, 6)
    for dim, shards_of in cuts:
        steps = jnp.exp(jax.random.uniform(jax.random.fold_in(own, dim), (shards_of,), jnp.float32, low / len(cuts), top_value / len(cuts)))
        gain = gain * jnp.repeat(steps, dims[dim] // shards_of).reshape([-1 if axis == dim else 1 for axis in range(len(dims))])
    return gain


def split_up(number_of, total, reach, lean):
    loads = [(1 << 20) // math.isqrt(standing ** lean) + 1 for standing in range(2, number_of + 1)]
    spare, counts = total - reach - (number_of - 1), [1] * (number_of - 1)
    while spare > 0:
        candidates = [i for i in range(number_of - 1) if counts[i] < reach]
        mass, budget = sum([loads[i] for i in candidates]), spare
        for i in candidates:
            addition = min(reach - counts[i], max(1, budget * loads[i] // mass), spare)
            counts[i] = counts[i] + addition
            spare = spare - addition
    return np.array([reach] + counts)


def ragged_sizes(rng, amount, total, limit, slope):
    if amount == 2:
        one = jax.random.randint(rng, (), max(1, total - limit), min(limit, total - 1) + 1)
        return jnp.stack([one, total - one])
    lengths = jnp.asarray(split_up(amount, total, limit, slope), jnp.int32)
    couples = (amount - 1) // 2
    source_of, receiver = lengths[1:1 + 2 * couples:2], lengths[2:2 + 2 * couples:2]
    margin = jnp.minimum(source_of - 1, limit - receiver)
    moved = jax.random.randint(jax.random.fold_in(rng, 1), (couples,), 0, 1 << 20) % (margin + 1)
    lengths = lengths.at[1:1 + 2 * couples:2].set(source_of - moved).at[2:2 + 2 * couples:2].set(receiver + moved)
    return lengths[jax.random.permutation(jax.random.fold_in(rng, 2), amount)]


def noise(rng, dims, spread, limit, cuts=(), held_as=jnp.bfloat16):
    entries = spread * jax.random.normal(rng, dims, jnp.float32)
    if cuts:
        entries = entries * block_levels(rng, dims, cuts, -0.22, 0.18)
    return jnp.clip(entries, -limit, limit).astype(held_as)


def bell_draw_with(rng, extent, width, bound, cuts, heavy, held_as=jnp.bfloat16):
    result = width * jax.random.normal(rng, extent, jnp.float32)
    if cuts:
        result = result * block_levels(rng, extent, cuts, -0.22, 0.18)
    return jnp.clip(raised(result, jax.random.fold_in(rng, 3), *heavy), -bound, bound).astype(held_as)


def setup_inputs(seed: int = 0) -> dict:
    seeds = jax.random.split(jax.random.key(seed), 6)
    spec = bell_draw_with(seeds[0], (2, FIELDS, LEVELS, MW, MW), (2 * MW * MW) ** -0.5, 0.0048828125, ((2, 16), (3, 32)), (4, 2, 16, 2.0))
    legendre = noise(seeds[1], (MW, MW, PAIRS), 1.0, 4.0, ((0, 32), (1, 16)))
    mids = jax.random.permutation(seeds[2], MW).astype(jnp.int32)
    band_lats = ragged_sizes(seeds[3], N_WAVE, LATS, LAT_MAX, 2).astype(jnp.int32)
    nlon = draw_nlon(jax.random.fold_in(seeds[5], 71), 0)
    return {"spec": spec, "legendre": legendre, "mids": mids, "band_lats": band_lats, "nlon": nlon}


TWO_PI = 6.283185307179586


def angle_of(integer_steps, cycle_points):
    return integer_steps.astype(jnp.float32) * (TWO_PI / cycle_points.astype(jnp.float32))


def synthesize(channel_rows, wavenumbers, cycle_points):
    wave_total = wavenumbers.shape[0]
    coarse = jnp.arange(KH, dtype=jnp.int32)
    fine_steps = jnp.arange(128, dtype=jnp.int32)
    coarse_angle = angle_of((128 * wavenumbers[None, :] * coarse[:, None]) % cycle_points, cycle_points)
    cos_coarse = jnp.cos(coarse_angle)
    sin_coarse = jnp.sin(coarse_angle)
    real_part = channel_rows[:, :wave_total].astype(jnp.float32)
    imag_part = channel_rows[:, wave_total:].astype(jnp.float32)
    shifted_re = real_part[None] * cos_coarse[:, None, :] - imag_part[None] * sin_coarse[:, None, :]
    shifted_im = real_part[None] * sin_coarse[:, None, :] + imag_part[None] * cos_coarse[:, None, :]
    modulated = jnp.concatenate([shifted_re, shifted_im], axis=2).astype(jnp.bfloat16)
    fine_angle = angle_of((wavenumbers[:, None] * fine_steps[None, :]) % cycle_points, cycle_points)
    weight = jnp.where(wavenumbers == 0, 1.0, 2.0)
    weight = jnp.where(2 * wavenumbers < cycle_points, weight, 0.0).astype(jnp.bfloat16)
    twiddle_c = jnp.cos(fine_angle).astype(jnp.bfloat16) * weight[:, None]
    twiddle_s = jnp.sin(fine_angle).astype(jnp.bfloat16) * weight[:, None]
    twiddles = jnp.concatenate([twiddle_c, -twiddle_s], axis=0)
    channels = channel_rows.shape[0]
    product = jnp.dot(modulated.reshape(KH * channels, 2 * wave_total), twiddles, preferred_element_type=jnp.float32)
    product = jnp.transpose(product.reshape(KH, channels, 128), (1, 0, 2)).reshape(channels, KH * 128)
    product = product[:, :NLON_MAX]
    inside = jnp.arange(NLON_MAX, dtype=jnp.int32) < cycle_points
    return jnp.where(inside[None, :], product, 0.0).astype(jnp.bfloat16)


def reference(spec, legendre, mids, band_lats, nlon):
    degree = jnp.arange(MW, dtype=jnp.int32)
    per_block = MW // N_LEV

    def legendre_block(position):
        first_slot = (position * 16).astype(jnp.int32)
        coeffs = lax.dynamic_slice_in_dim(spec, first_slot, 16, 3).astype(jnp.float32)
        tables = lax.dynamic_slice_in_dim(legendre, first_slot, 16, 0).astype(jnp.float32)
        wavenumbers = lax.dynamic_slice_in_dim(mids, first_slot, 16, 0)
        present = degree[None, :] >= wavenumbers[:, None]
        coeffs = jnp.where(present[None, None, None], coeffs, 0.0)
        signs = 1.0 - 2.0 * ((degree[None, :] + wavenumbers[:, None]) % 2).astype(jnp.float32)
        southern = (tables * signs[:, :, None])[:, :, ::-1]
        stacked = jnp.concatenate([tables, southern], axis=2)
        coeffs = coeffs.reshape(coeffs.shape[:4] + (N_LEV, per_block))
        stacked = stacked.reshape(16, N_LEV, per_block, LATS)
        blocks = jnp.einsum("cflsbp,sbpq->bsqflc", coeffs, stacked).astype(jnp.bfloat16)
        return jnp.sum(blocks.astype(jnp.float32), axis=0)

    sums = lax.map(legendre_block, jnp.arange(MW // 16, dtype=jnp.int32))
    sums = sums.reshape(MW, LATS, FIELDS, LEVELS, 2).astype(jnp.bfloat16)
    sums = jnp.transpose(sums, (1, 2, 3, 4, 0)).reshape(LATS, FIELDS * LEVELS, 2 * MW)
    lat_ids = jnp.arange(LATS, dtype=jnp.int32)
    pair_of = jnp.where(lat_ids < PAIRS, lat_ids, LATS - 1 - lat_ids)
    lat_points = nlon[pair_of]

    def one_latitude(position):
        return synthesize(sums[position], mids, lat_points[position])

    lat_grid = lax.map(one_latitude, lat_ids)
    starts = jnp.cumsum(band_lats) - band_lats
    slot_ids = jnp.arange(LAT_MAX, dtype=jnp.int32)
    wanted = starts[:, None] + slot_ids[None, :]
    filled = slot_ids[None, :] < band_lats[:, None]
    slot_rows = lat_grid[jnp.minimum(wanted, LATS - 1)]
    slot_rows = jnp.where(filled[:, :, None, None], slot_rows, jnp.zeros((), jnp.bfloat16))
    return slot_rows.reshape(N_WAVE * LAT_MAX, FIELDS, LEVELS, NLON_MAX)
```

```python
import jax
import jax.numpy as jnp
from jax import lax
from jax.experimental import pallas as pl
from jax.experimental.pallas import tpu as pltpu
from jax.sharding import PartitionSpec as P

LAT_MAX = 8
NLON_MAX = 5136
KH = 41
WAVES = 32
LEVS = 16
CHIPS = 8
SLOTS = 40
GROUP = 5
MW = 1280
HALF = 640
BLOCK = 80
PAIRS = 64
LATS = 128
TWO_PI = 6.283185307179586
F32 = jnp.float32
BF16 = jnp.bfloat16
MESH = pl.DeviceIdType.MESH

SIN = []
_term = TWO_PI
for _i in range(6):
    SIN.append(_term)
    _term = -_term * TWO_PI * TWO_PI / ((2 * _i + 2) * (2 * _i + 3))


def quarter_sine(y):
    y2 = y * y
    acc = jnp.full_like(y2, SIN[-1])
    for c in SIN[-2::-1]:
        acc = acc * y2 + c
    return acc * y


def cos_sin(steps, cycle, inverse):
    rest = steps - jnp.floor(steps * inverse + 0.5) * cycle
    t = rest * inverse
    a = jnp.abs(t)
    folded = jnp.where(a > 0.25, jnp.where(t < 0, -0.5, 0.5) - t, t)
    return quarter_sine(0.25 - a), quarter_sine(folded)


def nt_dot(a, b):
    return lax.dot_general(a, b, (((1,), (1,)), ((), ())), preferred_element_type=F32)


def kernel(
    mids_ref, bands_ref, nlon_ref, spec_ref, leg_ref, mrow_ref, out_ref,
    spec_f, send_s, send_l, recv_s, recv_l, rhs, sums, send_r, recv_x,
    onehot, send_y, recv_z, zf, zs, expand, mcol, cosc, sinc, tw, mod, lat,
    ss_send, ss_recv, sl_send, sl_recv, sx_send, sx_recv, sz_send, sz_recv,
):
    w = lax.axis_index("wave")
    me = lax.axis_index("lev")
    z = me // 2
    c = me - 2 * z
    half = z // 4

    barrier = pltpu.get_barrier_semaphore()

    def greet_lev(k, carry):
        pl.semaphore_signal(barrier, inc=1, device_id={"lev": lax.rem(me + k, LEVS)}, device_id_type=MESH)
        return carry

    def greet_wave(k, carry):
        pl.semaphore_signal(barrier, inc=1, device_id={"wave": lax.rem(w + k, WAVES)}, device_id_type=MESH)
        return carry

    lax.fori_loop(1, LEVS, greet_lev, 0)
    lax.fori_loop(1, WAVES, greet_wave, 0)

    for tile in range(10):
        spec_f[tile, 0:240, :] = spec_ref[:, 128 * tile:128 * tile + 128].astype(F32)
        spec_f[tile, 240:256, :] = jnp.zeros((16, 128), F32)

    unit = jnp.where(
        lax.broadcasted_iota(jnp.int32, (BLOCK, BLOCK), 0) == lax.broadcasted_iota(jnp.int32, (BLOCK, BLOCK), 1),
        1.0, 0.0,
    ).astype(BF16)

    pl.semaphore_wait(barrier, LEVS + WAVES - 2)

    def spec_copy(k, h):
        to = lax.rem(z + k, CHIPS)
        return pltpu.make_async_remote_copy(
            src_ref=send_s.at[to, h], dst_ref=recv_s.at[me], send_sem=ss_send.at[2 * k + h],
            recv_sem=ss_recv.at[me], device_id={"lev": 2 * to + h}, device_id_type=MESH,
        )

    def leg_copy(k):
        to = lax.rem(z + k, CHIPS)
        return pltpu.make_async_remote_copy(
            src_ref=send_l.at[to], dst_ref=recv_l.at[lax.rem(me, 8)], send_sem=sl_send.at[k],
            recv_sem=sl_recv.at[lax.rem(me, 8)], device_id={"lev": 2 * to + half}, device_id_type=MESH,
        )

    def prepare(k):
        to = lax.rem(z + k, CHIPS)
        for tile in range(10):
            rows = spec_f[tile, pl.ds(to, 32, stride=8), :].astype(BF16)
            send_s[to, tile // 5, :, 128 * (tile % 5):128 * (tile % 5) + 128] = rows
        for p in range(3):
            first = leg_ref[16 * p + to]
            second = leg_ref[16 * p + 8 + to] if p < 2 else jnp.zeros((PAIRS, BLOCK), BF16)
            stacked = jnp.concatenate([first, second], axis=0)
            send_l[to, BLOCK * p:BLOCK * p + BLOCK, :] = nt_dot(unit, stacked).astype(BF16)

    def send_far(i, carry):
        k = CHIPS - i
        prepare(k)
        for h in range(2):
            spec_copy(k, h).start()
        leg_copy(k).start()
        return carry

    lax.fori_loop(1, CHIPS, send_far, 0)
    prepare(0)
    for h in range(2):
        @pl.when(c == h)
        def _():
            pltpu.make_async_copy(send_s.at[z, h], recv_s.at[me], ss_recv.at[me]).start()

        @pl.when(c != h)
        def _():
            spec_copy(0, h).start()

    @pl.when(c == half)
    def _():
        pltpu.make_async_copy(send_l.at[z], recv_l.at[lax.rem(me, 8)], sl_recv.at[lax.rem(me, 8)]).start()

    @pl.when(c != half)
    def _():
        leg_copy(0).start()

    start = jnp.int32(0)
    own_start = jnp.int32(0)
    sub16 = lax.broadcasted_iota(jnp.int32, (16, 256), 0)
    lane = lax.broadcasted_iota(jnp.int32, (16, 256), 1)
    lat_of = jnp.where(lane < 128, lane & 63, 127 - (lane & 63))
    for e in range(WAVES // 2):
        count_a, count_b = bands_ref[2 * e], bands_ref[2 * e + 1]
        start_b = start + count_a
        own_start = jnp.where(w == 2 * e, start, jnp.where(w == 2 * e + 1, start_b, own_start))
        inner = sub16 & 7
        wanted = jnp.where(sub16 < 8, start, start_b) + inner
        filled = inner < jnp.where(sub16 < 8, count_a, count_b)
        match = jnp.where(filled, wanted, -1) == lat_of
        onehot[16 * e:16 * e + 16, :] = jnp.where(match, 1.0, 0.0).astype(BF16)
        start = start_b + count_b

    def cycle_of(slot):
        latitude = jnp.minimum(own_start + slot, LATS - 1)
        pair = jnp.where(latitude < PAIRS, latitude, LATS - 1 - latitude)
        return nlon_ref[pair]

    krow = lax.broadcasted_iota(jnp.int32, (128, 256), 0)
    klane = lax.broadcasted_iota(jnp.int32, (128, 256), 1)
    col = klane & 127
    channel = jnp.where(col >= KH, 1, 0) + jnp.where(col >= 2 * KH, 1, 0) + jnp.where(col >= 3 * KH, 100, 0)
    base = krow - (GROUP * channel + jnp.where(klane >= 128, 15, 0))

    def fill_expand(i, carry):
        zl = i // GROUP
        match = base == zl * 32 + (i - GROUP * zl)
        expand[i] = jnp.where(match, 1.0, 0.0).astype(BF16)
        return carry

    lax.fori_loop(0, 20, fill_expand, 0)

    for t in range(10):
        row = jnp.broadcast_to(mrow_ref[0:1, 128 * t:128 * t + 128], (128, 128))
        mcol[128 * t:128 * t + 128, :] = row.T

    col1 = lax.broadcasted_iota(jnp.int32, (1, 128), 1)
    channel1 = jnp.where(col1 >= KH, 1, 0) + jnp.where(col1 >= 2 * KH, 1, 0)
    coarse_steps = (128 * (col1 - KH * channel1)).astype(F32)
    a_steps = (16 * lax.broadcasted_iota(jnp.int32, (8, 128), 0)).astype(F32)
    b_steps = lax.broadcasted_iota(jnp.int32, (16, 128), 0).astype(F32)

    def tables(slot, carry):
        cycle = jnp.full((1, 128), cycle_of(slot), jnp.int32).astype(F32)
        inverse = 1.0 / cycle

        def coarse(i, inner_carry):
            at = pl.multiple_of(128 * i, 128)
            cos_part, sin_part = cos_sin(mcol[pl.ds(at, 128), :] * coarse_steps, cycle, inverse)
            cosc[slot, pl.ds(at, 128), :] = cos_part
            sinc[slot, pl.ds(at, 128), :] = sin_part
            return inner_carry

        lax.fori_loop(0, 10, coarse, 0)

        def fine(i, inner_carry):
            at = pl.multiple_of(128 * i, 128)
            m = mrow_ref[0:1, pl.ds(at, 128)]
            weight = jnp.where(m == 0, 1.0, 2.0)
            weight = jnp.where(2 * m < cycle, weight, 0.0)
            cos_a, sin_a = cos_sin(m * a_steps, cycle, inverse)
            cos_b, sin_b = cos_sin(m * b_steps, cycle, inverse)
            cos_a = cos_a * weight
            sin_a = sin_a * weight
            for a in range(8):
                ca, sa = cos_a[a:a + 1, :], sin_a[a:a + 1, :]
                tw[slot, 16 * a:16 * a + 16, pl.ds(at, 128)] = (ca * cos_b - sa * sin_b).astype(BF16)
                other = pl.multiple_of(at + MW, 128)
                tw[slot, 16 * a:16 * a + 16, pl.ds(other, 128)] = (-(sa * cos_b + ca * sin_b)).astype(BF16)
            return inner_carry

        lax.fori_loop(0, 10, fine, 0)
        return carry

    lax.fori_loop(0, LAT_MAX, tables, 0)

    def wait_spec(k, carry):
        pltpu.make_async_copy(recv_s.at[k], recv_s.at[k], ss_recv.at[k]).wait()
        return carry

    def wait_leg(k, carry):
        pltpu.make_async_copy(recv_l.at[k], recv_l.at[k], sl_recv.at[k]).wait()
        return carry

    lax.fori_loop(0, LEVS, wait_spec, 0)
    lax.fori_loop(0, 8, wait_leg, 0)

    left = recv_s[...].reshape(512, HALF)
    row_r = lax.broadcasted_iota(jnp.int32, (512, 256), 0) & 31
    j_r = row_r - GROUP * jnp.floor((row_r.astype(F32) + 0.5) * 0.2).astype(jnp.int32)
    lane_r = lax.broadcasted_iota(jnp.int32, (512, 256), 1)
    degree = lax.broadcasted_iota(jnp.int32, (HALF, 128), 0) + HALF * c
    lane_n = lax.broadcasted_iota(jnp.int32, (HALF, 128), 1)
    for p in range(3):
        m_a = mids_ref[SLOTS * w + 16 * p + z]
        m_b = mids_ref[SLOTS * w + 16 * p + 8 + z] if p < 2 else m_a
        m = jnp.where(lane_n < PAIRS, m_a, m_b)
        table = recv_l[:, BLOCK * p:BLOCK * p + BLOCK, :].reshape(HALF, 128).astype(F32)
        table = jnp.where(degree >= m, table, 0.0)
        rhs[:, 0:128] = table.astype(BF16)
        rhs[:, 128:256] = jnp.where(((degree + m) & 1) == 1, -table, table).astype(BF16)
        terms = jnp.dot(left, rhs[...], preferred_element_type=F32)
        if p == 0:
            sums[...] = terms
        else:
            sums[...] = jnp.where(j_r >= 2 * p, terms, sums[...])
    keep = ((lane_r & 127) < PAIRS) == ((j_r & 1) == 0)
    send_r[...] = jnp.where(keep, sums[...], 0.0).astype(BF16).reshape(LEVS, 32, 256)

    def level_copy(k):
        to = lax.rem(me + k, LEVS)
        return pltpu.make_async_remote_copy(
            src_ref=send_r.at[to], dst_ref=recv_x.at[me], send_sem=sx_send.at[k],
            recv_sem=sx_recv.at[me], device_id={"lev": to}, device_id_type=MESH,
        )

    def send_level(k, carry):
        level_copy(k).start()
        return carry

    lax.fori_loop(1, LEVS, send_level, 0)
    pltpu.make_async_copy(send_r.at[me], recv_x.at[me], sx_recv.at[me]).start()

    def wait_level(k, carry):
        pltpu.make_async_copy(recv_x.at[k], recv_x.at[k], sx_recv.at[k]).wait()
        return carry

    lax.fori_loop(0, LEVS, wait_level, 0)

    got = recv_x[...].astype(F32).reshape(CHIPS, 2, 32, 256)
    level_sums = (got[:, 0] + got[:, 1]).reshape(256, 256).astype(BF16)
    by_slot = nt_dot(onehot[...], level_sums)
    low = by_slot[:, 0:128].reshape(WAVES, 8, 128)
    high = by_slot[:, 128:256].reshape(WAVES, 8, 128)
    send_y[...] = jnp.concatenate([low, high], axis=1).astype(BF16)

    def band_copy(k):
        to = lax.rem(w + k, WAVES)
        return pltpu.make_async_remote_copy(
            src_ref=send_y.at[to], dst_ref=recv_z.at[w], send_sem=sz_send.at[k],
            recv_sem=sz_recv.at[w], device_id={"wave": to}, device_id_type=MESH,
        )

    def send_band(k, carry):
        band_copy(k).start()
        return carry

    lax.fori_loop(1, WAVES, send_band, 0)
    pltpu.make_async_copy(send_y.at[w], recv_z.at[w], sz_recv.at[w]).start()

    def wait_band(k, carry):
        pltpu.make_async_copy(recv_z.at[k], recv_z.at[k], sz_recv.at[k]).wait()
        return carry

    lax.fori_loop(0, WAVES, wait_band, 0)

    zf[...] = recv_z[...].astype(F32).reshape(512, 128)
    for slot in range(LAT_MAX):
        zs[64 * slot:64 * slot + 64, :] = zf[pl.ds(slot, 64, stride=8), :].astype(BF16)

    def modulate(i, carry):
        both = jnp.dot(zs[...], expand[i], preferred_element_type=F32)
        at = pl.multiple_of(64 * i, 64)
        other = pl.multiple_of(64 * i + MW, 64)
        for slot in range(LAT_MAX):
            re = both[64 * slot:64 * slot + 64, 0:128]
            im = both[64 * slot:64 * slot + 64, 128:256]
            cos_part = cosc[slot, pl.ds(at, 64), :]
            sin_part = sinc[slot, pl.ds(at, 64), :]
            mod[slot, pl.ds(at, 64), :] = (re * cos_part - im * sin_part).astype(BF16)
            mod[slot, pl.ds(other, 64), :] = (re * sin_part + im * cos_part).astype(BF16)
        return carry

    lax.fori_loop(0, 20, modulate, 0)

    def transform(slot, carry):
        points = jnp.dot(tw[slot], mod[slot], preferred_element_type=F32)
        lat[pl.ds(slot, 128, stride=8), :] = points.T
        return carry

    lax.fori_loop(0, LAT_MAX, transform, 0)

    slot_of = lax.broadcasted_iota(jnp.int32, (8, 128), 0)
    lon = lax.broadcasted_iota(jnp.int32, (8, 128), 1)
    cycles = jnp.zeros((8, 128), jnp.int32)
    for slot in range(LAT_MAX):
        cycles = jnp.where(slot_of == slot, cycle_of(slot), cycles)
    for f in range(3):
        for kh in range(KH):
            at = 8 * (KH * f + kh)
            width = min(128, NLON_MAX - 128 * kh)
            tile = jnp.where(lon + 128 * kh < cycles, lat[at:at + 8, :], 0.0).astype(BF16)
            out_ref[f, :, 128 * kh:128 * kh + width] = tile[:, 0:width]

    def sent_far(k, carry):
        for h in range(2):
            spec_copy(k, h).wait_send()
        leg_copy(k).wait_send()
        return carry

    lax.fori_loop(1, CHIPS, sent_far, 0)
    for h in range(2):
        @pl.when(c != h)
        def _():
            spec_copy(0, h).wait_send()

    @pl.when(c != half)
    def _():
        leg_copy(0).wait_send()

    def sent_level(k, carry):
        level_copy(k).wait_send()
        return carry

    lax.fori_loop(1, LEVS, sent_level, 0)

    def sent_band(k, carry):
        band_copy(k).wait_send()
        return carry

    lax.fori_loop(1, WAVES, sent_band, 0)


def on_device(spec, legendre, mids, band_lats, nlon):
    spec_rows = spec.reshape(240, MW)
    tables = jnp.transpose(legendre, (0, 2, 1))
    order = jnp.transpose(mids.reshape(WAVES, GROUP, 2, 4), (3, 1, 0, 2)).reshape(1, MW).astype(F32)
    smem = pl.BlockSpec(memory_space=pltpu.SMEM)
    vmem = pl.BlockSpec(memory_space=pltpu.VMEM)
    dma = pltpu.SemaphoreType.DMA
    planes = pl.pallas_call(
        kernel,
        out_shape=jax.ShapeDtypeStruct((3, LAT_MAX, NLON_MAX), BF16),
        in_specs=[smem, smem, smem, vmem, vmem, vmem],
        out_specs=vmem,
        scratch_shapes=[
            pltpu.VMEM((10, 256, 128), F32),
            pltpu.VMEM((CHIPS, 2, 32, HALF), BF16),
            pltpu.VMEM((CHIPS, 3 * BLOCK, 128), BF16),
            pltpu.VMEM((LEVS, 32, HALF), BF16),
            pltpu.VMEM((8, 3 * BLOCK, 128), BF16),
            pltpu.VMEM((HALF, 256), BF16),
            pltpu.VMEM((512, 256), F32),
            pltpu.VMEM((LEVS, 32, 256), BF16),
            pltpu.VMEM((LEVS, 32, 256), BF16),
            pltpu.VMEM((256, 256), BF16),
            pltpu.VMEM((WAVES, 16, 128), BF16),
            pltpu.VMEM((WAVES, 16, 128), BF16),
            pltpu.VMEM((512, 128), F32),
            pltpu.VMEM((512, 128), BF16),
            pltpu.VMEM((20, 128, 256), BF16),
            pltpu.VMEM((MW, 128), F32),
            pltpu.VMEM((LAT_MAX, MW, 128), F32),
            pltpu.VMEM((LAT_MAX, MW, 128), F32),
            pltpu.VMEM((LAT_MAX, 128, 2 * MW), BF16),
            pltpu.VMEM((LAT_MAX, 2 * MW, 128), BF16),
            pltpu.VMEM((1024, 128), F32),
            dma((2 * CHIPS,)), dma((LEVS,)), dma((CHIPS,)), dma((8,)),
            dma((LEVS,)), dma((LEVS,)), dma((WAVES,)), dma((WAVES,)),
        ],
        compiler_params=pltpu.CompilerParams(
            collective_id=0, has_side_effects=True, vmem_limit_bytes=52 * 2**20
        ),
    )(mids, band_lats, nlon, spec_rows, tables, order)
    return jnp.transpose(planes, (1, 0, 2)).reshape(LAT_MAX, 3, 1, NLON_MAX)


def solution(mesh):
    in_specs = (P(None, None, "lev", "wave", None), P("wave", "lev", None), P(), P(), P())
    out_specs = P("wave", None, "lev", None)
    return jax.shard_map(
        on_device, mesh=mesh, in_specs=in_specs, out_specs=out_specs, check_vma=False
    )
```

```python
import jax
import jax.numpy as jnp
from jax import lax
from jax.experimental import pallas as pl
from jax.experimental.pallas import tpu as pltpu
from jax.sharding import PartitionSpec as P

LAT_MAX = 8
NLON_MAX = 5136
KH = 41
WAVES = 32
LEVS = 16
CHIPS = 8
SLOTS = 40
GROUP = 5
MW = 1280
HALF = 640
BLOCK = 80
LEG_ROWS = 208
PAIRS = 64
LATS = 128
TWO_PI = 6.283185307179586
F32 = jnp.float32
BF16 = jnp.bfloat16
MESH = pl.DeviceIdType.MESH

SIN = []
_term = TWO_PI
for _i in range(6):
    SIN.append(_term)
    _term = -_term * TWO_PI * TWO_PI / ((2 * _i + 2) * (2 * _i + 3))


def quarter_sine(y):
    y2 = y * y
    acc = jnp.full_like(y2, SIN[-1])
    for c in SIN[-2::-1]:
        acc = acc * y2 + c
    return acc * y


def cos_sin(steps, cycle, inverse):
    rest = steps - jnp.floor(steps * inverse + 0.5) * cycle
    t = rest * inverse
    a = jnp.abs(t)
    folded = jnp.where(a > 0.25, jnp.where(t < 0, -0.5, 0.5) - t, t)
    return quarter_sine(0.25 - a), quarter_sine(folded)


def nt_dot(a, b):
    return lax.dot_general(a, b, (((1,), (1,)), ((), ())), preferred_element_type=F32)


def kernel(
    mids_hbm, bands_hbm, nlon_hbm, spec_hbm, leg_hbm, mids_rows_hbm, out_ref,
    mids_ref, bands_ref, nlon_ref, spec_ref, leg_ref, mids_rows, mrow_ref, spec_f, send_s, send_l, recv_s, recv_l, rhs, sums, send_r, recv_x,
    onehot, send_y, recv_z, zf, zs, expand, mcol, cosc, sinc, tw, mod, lat,
    load_sem, ss_send, ss_recv, sl_send, sl_recv, sx_send, sx_recv, sz_send, sz_recv,
):
    w = lax.axis_index("wave")
    me = lax.axis_index("lev")
    z = me // 2
    c = me - 2 * z
    half = z // 4

    barrier = pltpu.get_barrier_semaphore()
    for k in range(1, LEVS):
        pl.semaphore_signal(barrier, inc=1, device_id={"lev": lax.rem(me + k, LEVS)}, device_id_type=MESH)
    for k in range(1, WAVES):
        pl.semaphore_signal(barrier, inc=1, device_id={"wave": lax.rem(w + k, WAVES)}, device_id_type=MESH)

    mids_rows[...] = jnp.zeros_like(mids_rows)
    loads = [
        pltpu.make_async_copy(spec_hbm, spec_ref, load_sem.at[0]),
        pltpu.make_async_copy(leg_hbm, leg_ref, load_sem.at[1]),
        pltpu.make_async_copy(mids_rows_hbm, mids_rows.at[0:10], load_sem.at[2]),
        pltpu.make_async_copy(mids_hbm, mids_ref, load_sem.at[3]),
        pltpu.make_async_copy(bands_hbm, bands_ref, load_sem.at[4]),
        pltpu.make_async_copy(nlon_hbm, nlon_ref, load_sem.at[5]),
    ]
    for load in loads:
        load.start()
    loads[0].wait()

    for tile in range(10):
        spec_f[tile, 0:240, :] = spec_ref[:, 128 * tile:128 * tile + 128].astype(F32)
        spec_f[tile, 240:256, :] = jnp.zeros((16, 128), F32)

    unit = jnp.where(
        lax.broadcasted_iota(jnp.int32, (BLOCK, BLOCK), 0) == lax.broadcasted_iota(jnp.int32, (BLOCK, BLOCK), 1),
        1.0, 0.0,
    ).astype(BF16)

    fold = jnp.where(
        (lax.broadcasted_iota(jnp.int32, (48, BLOCK), 0) == lax.broadcasted_iota(jnp.int32, (48, BLOCK), 1))
        | (lax.broadcasted_iota(jnp.int32, (48, BLOCK), 0) + 40 == lax.broadcasted_iota(jnp.int32, (48, BLOCK), 1)),
        1.0, 0.0,
    )
    fold = jnp.where(lax.broadcasted_iota(jnp.int32, (48, BLOCK), 0) < 40, fold, 0.0).astype(BF16)
    upper = (lax.broadcasted_iota(jnp.int32, (LATS, BLOCK), 0) < PAIRS) == (
        lax.broadcasted_iota(jnp.int32, (LATS, BLOCK), 1) < 40
    )
    loads[1].wait()
    pl.semaphore_wait(barrier, LEVS + WAVES - 2)

    def spec_copy(k, h):
        to = lax.rem(z + k, CHIPS)
        return pltpu.make_async_remote_copy(
            src_ref=send_s.at[to, h], dst_ref=recv_s.at[me], send_sem=ss_send,
            recv_sem=ss_recv, device_id={"lev": 2 * to + h}, device_id_type=MESH,
        )

    def leg_copy(k):
        to = lax.rem(z + k, CHIPS)
        return pltpu.make_async_remote_copy(
            src_ref=send_l.at[to], dst_ref=recv_l.at[lax.rem(me, 8)], send_sem=sl_send,
            recv_sem=sl_recv, device_id={"lev": 2 * to + half}, device_id_type=MESH,
        )

    def prepare(k):
        to = lax.rem(z + k, CHIPS)
        for tile in range(10):
            rows = spec_f[tile, pl.ds(to, 32, stride=8), :].astype(BF16)
            send_s[to, tile // 5, :, 128 * (tile % 5):128 * (tile % 5) + 128] = rows
        for p in range(2):
            stacked = jnp.concatenate([leg_ref[16 * p + to], leg_ref[16 * p + 8 + to]], axis=0)
            send_l[to, BLOCK * p:BLOCK * p + BLOCK, :] = nt_dot(unit, stacked).astype(BF16)
        last = leg_ref[32 + to].astype(F32)
        stacked = jnp.where(upper, jnp.concatenate([last, last], axis=0), 0.0).astype(BF16)
        send_l[to, 2 * BLOCK:LEG_ROWS, :] = nt_dot(fold, stacked).astype(BF16)

    def send_far(i, carry):
        k = jnp.where(lax.rem(i, 2) == 1, 4 - (i + 1) // 2, 4 + i // 2)
        prepare(k)
        for h in range(2):
            spec_copy(k, h).start()
        leg_copy(k).start()
        return carry

    lax.fori_loop(0, CHIPS - 1, send_far, 0)
    prepare(0)
    for h in range(2):
        @pl.when(c == h)
        def _():
            pltpu.make_async_copy(send_s.at[z, h], recv_s.at[me], ss_recv).start()

        @pl.when(c != h)
        def _():
            spec_copy(0, h).start()

    @pl.when(c == half)
    def _():
        pltpu.make_async_copy(send_l.at[z], recv_l.at[lax.rem(me, 8)], sl_recv).start()

    @pl.when(c != half)
    def _():
        leg_copy(0).start()

    for load in loads[2:]:
        load.wait()

    start = jnp.int32(0)
    own_start = jnp.int32(0)
    sub16 = lax.broadcasted_iota(jnp.int32, (16, 256), 0)
    lane = lax.broadcasted_iota(jnp.int32, (16, 256), 1)
    lat_of = jnp.where(lane < 128, lane & 63, 127 - (lane & 63))
    for e in range(WAVES // 2):
        count_a, count_b = bands_ref[2 * e], bands_ref[2 * e + 1]
        start_b = start + count_a
        own_start = jnp.where(w == 2 * e, start, jnp.where(w == 2 * e + 1, start_b, own_start))
        inner = sub16 & 7
        wanted = jnp.where(sub16 < 8, start, start_b) + inner
        filled = inner < jnp.where(sub16 < 8, count_a, count_b)
        match = jnp.where(filled, wanted, -1) == lat_of
        onehot[16 * e:16 * e + 16, :] = jnp.where(match, 1.0, 0.0).astype(BF16)
        start = start_b + count_b

    def cycle_of(slot):
        latitude = jnp.minimum(own_start + slot, LATS - 1)
        pair = jnp.where(latitude < PAIRS, latitude, LATS - 1 - latitude)
        return nlon_ref[pair]

    krow = lax.broadcasted_iota(jnp.int32, (128, 256), 0)
    klane = lax.broadcasted_iota(jnp.int32, (128, 256), 1)
    col = klane & 127
    channel = jnp.where(col >= KH, 1, 0) + jnp.where(col >= 2 * KH, 1, 0) + jnp.where(col >= 3 * KH, 100, 0)
    base = krow - (GROUP * channel + jnp.where(klane >= 128, 15, 0))

    def fill_expand(i, carry):
        zl = i // GROUP
        match = base == zl * 32 + (i - GROUP * zl)
        expand[i] = jnp.where(match, 1.0, 0.0).astype(BF16)
        return carry

    lax.fori_loop(0, 20, fill_expand, 0)

    natural = mids_rows[...].astype(F32)
    high = jnp.floor(natural * 0.125)
    digits = jnp.concatenate([high, natural - 8.0 * high], axis=0).astype(BF16)
    for t in range(10):
        place = lax.broadcasted_iota(jnp.int32, (128, 128), 1) + 128 * t
        group = place >> 6
        zl = jnp.where(group >= 5, 1, 0) + jnp.where(group >= 10, 1, 0) + jnp.where(group >= 15, 1, 0)
        source = SLOTS * ((place & 63) >> 1) + 8 * (group - GROUP * zl) + 4 * (place & 1) + zl
        pick = lax.broadcasted_iota(jnp.int32, (128, 128), 0) == (source & 127)
        found = jnp.dot(digits, jnp.where(pick, 1.0, 0.0).astype(BF16), preferred_element_type=F32)
        found = 8.0 * found[0:16, :] + found[16:32, :]
        here = lax.broadcasted_iota(jnp.int32, (16, 128), 0) == (source[0:16, :] >> 7)
        row = jnp.sum(jnp.where(here, found, 0.0), axis=0, keepdims=True)
        mrow_ref[0:1, 128 * t:128 * t + 128] = row
        mcol[128 * t:128 * t + 128, :] = jnp.broadcast_to(row, (128, 128)).T

    col1 = lax.broadcasted_iota(jnp.int32, (1, 128), 1)
    channel1 = jnp.where(col1 >= KH, 1, 0) + jnp.where(col1 >= 2 * KH, 1, 0)
    coarse_steps = (128 * (col1 - KH * channel1)).astype(F32)
    a_steps = (16 * lax.broadcasted_iota(jnp.int32, (8, 128), 0)).astype(F32)
    b_steps = lax.broadcasted_iota(jnp.int32, (16, 128), 0).astype(F32)

    def tables(slot, carry):
        cycle = jnp.full((1, 128), cycle_of(slot), jnp.int32).astype(F32)
        inverse = 1.0 / cycle

        def coarse(i, inner_carry):
            at = pl.multiple_of(128 * i, 128)
            cos_part, sin_part = cos_sin(mcol[pl.ds(at, 128), :] * coarse_steps, cycle, inverse)
            cosc[slot, pl.ds(at, 128), :] = cos_part
            sinc[slot, pl.ds(at, 128), :] = sin_part
            return inner_carry

        lax.fori_loop(0, 10, coarse, 0)

        def fine(i, inner_carry):
            at = pl.multiple_of(128 * i, 128)
            m = mrow_ref[0:1, pl.ds(at, 128)]
            weight = jnp.where(m == 0, 1.0, 2.0)
            weight = jnp.where(2 * m < cycle, weight, 0.0)
            cos_a, sin_a = cos_sin(m * a_steps, cycle, inverse)
            cos_b, sin_b = cos_sin(m * b_steps, cycle, inverse)
            cos_a = cos_a * weight
            sin_a = sin_a * weight
            for a in range(8):
                ca, sa = cos_a[a:a + 1, :], sin_a[a:a + 1, :]
                tw[slot, 16 * a:16 * a + 16, pl.ds(at, 128)] = (ca * cos_b - sa * sin_b).astype(BF16)
                other = pl.multiple_of(at + MW, 128)
                tw[slot, 16 * a:16 * a + 16, pl.ds(other, 128)] = (-(sa * cos_b + ca * sin_b)).astype(BF16)
            return inner_carry

        lax.fori_loop(0, 10, fine, 0)
        return carry

    lax.fori_loop(0, LAT_MAX, tables, 0)

    pltpu.make_async_copy(recv_s, recv_s, ss_recv).wait()
    pltpu.make_async_copy(recv_l, recv_l, sl_recv).wait()

    left = recv_s[...].reshape(512, HALF)
    row_r = lax.broadcasted_iota(jnp.int32, (512, 256), 0) & 31
    j_r = row_r - GROUP * jnp.floor((row_r.astype(F32) + 0.5) * 0.2).astype(jnp.int32)
    lane_r = lax.broadcasted_iota(jnp.int32, (512, 256), 1)
    degree = lax.broadcasted_iota(jnp.int32, (HALF, 128), 0) + HALF * c
    lane_n = lax.broadcasted_iota(jnp.int32, (HALF, 128), 1)
    for p in range(3):
        m_a = mids_ref[SLOTS * w + 16 * p + z]
        m_b = mids_ref[SLOTS * w + 16 * p + 8 + z] if p < 2 else m_a
        m = jnp.where(lane_n < PAIRS, m_a, m_b)
        if p < 2:
            table = recv_l[:, BLOCK * p:BLOCK * p + BLOCK, :].astype(F32).reshape(HALF, 128)
        else:
            packed = recv_l[:, 2 * BLOCK:LEG_ROWS, :].astype(F32)
            swapped = jnp.concatenate([packed[:, :, 64:128], packed[:, :, 0:64]], axis=2)
            table = jnp.concatenate([packed[:, 0:40], swapped[:, 0:40]], axis=1).reshape(HALF, 128)
        table = jnp.where(degree >= m, table, 0.0)
        rhs[:, 0:128] = table.astype(BF16)
        rhs[:, 128:256] = jnp.where(((degree + m) & 1) == 1, -table, table).astype(BF16)
        terms = jnp.dot(left, rhs[...], preferred_element_type=F32)
        if p == 0:
            sums[...] = terms
        else:
            sums[...] = jnp.where(j_r >= 2 * p, terms, sums[...])
    keep = ((lane_r & 127) < PAIRS) == ((j_r & 1) == 0)
    send_r[...] = jnp.where(keep, sums[...], 0.0).astype(BF16).reshape(LEVS, 32, 256)

    def level_copy(k):
        to = lax.rem(me + k, LEVS)
        return pltpu.make_async_remote_copy(
            src_ref=send_r.at[to], dst_ref=recv_x.at[me], send_sem=sx_send,
            recv_sem=sx_recv, device_id={"lev": to}, device_id_type=MESH,
        )

    for k in sorted(range(1, LEVS), key=lambda k: abs(k - LEVS // 2)):
        level_copy(k).start()
    pltpu.make_async_copy(send_r.at[me], recv_x.at[me], sx_recv).start()
    pltpu.make_async_copy(recv_x, recv_x, sx_recv).wait()

    got = recv_x[...].astype(F32).reshape(CHIPS, 2, 32, 256)
    level_sums = (got[:, 0] + got[:, 1]).reshape(256, 256).astype(BF16)
    by_slot = nt_dot(onehot[...], level_sums)
    low = by_slot[:, 0:128].reshape(WAVES, 8, 128)
    high = by_slot[:, 128:256].reshape(WAVES, 8, 128)
    send_y[...] = jnp.concatenate([low, high], axis=1).astype(BF16)

    def band_copy(k):
        to = lax.rem(w + k, WAVES)
        return pltpu.make_async_remote_copy(
            src_ref=send_y.at[to], dst_ref=recv_z.at[w], send_sem=sz_send,
            recv_sem=sz_recv, device_id={"wave": to}, device_id_type=MESH,
        )

    for k in sorted(range(1, WAVES), key=lambda k: abs(k - WAVES // 2)):
        band_copy(k).start()
    pltpu.make_async_copy(send_y.at[w], recv_z.at[w], sz_recv).start()
    pltpu.make_async_copy(recv_z, recv_z, sz_recv).wait()

    zf[...] = recv_z[...].astype(F32).reshape(512, 128)
    for slot in range(LAT_MAX):
        zs[64 * slot:64 * slot + 64, :] = zf[pl.ds(slot, 64, stride=8), :].astype(BF16)

    def modulate(i, carry):
        both = jnp.dot(zs[...], expand[i], preferred_element_type=F32)
        at = pl.multiple_of(64 * i, 64)
        other = pl.multiple_of(64 * i + MW, 64)
        for slot in range(LAT_MAX):
            re = both[64 * slot:64 * slot + 64, 0:128]
            im = both[64 * slot:64 * slot + 64, 128:256]
            cos_part = cosc[slot, pl.ds(at, 64), :]
            sin_part = sinc[slot, pl.ds(at, 64), :]
            mod[slot, pl.ds(at, 64), :] = (re * cos_part - im * sin_part).astype(BF16)
            mod[slot, pl.ds(other, 64), :] = (re * sin_part + im * cos_part).astype(BF16)
        return carry

    lax.fori_loop(0, 20, modulate, 0)

    def transform(slot, carry):
        points = jnp.dot(tw[slot], mod[slot], preferred_element_type=F32)
        lat[pl.ds(slot, 128, stride=8), :] = points.T
        return carry

    lax.fori_loop(0, LAT_MAX, transform, 0)

    slot_of = lax.broadcasted_iota(jnp.int32, (8, 128), 0)
    lon = lax.broadcasted_iota(jnp.int32, (8, 128), 1)
    cycles = jnp.zeros((8, 128), jnp.int32)
    for slot in range(LAT_MAX):
        cycles = jnp.where(slot_of == slot, cycle_of(slot), cycles)
    for f in range(3):
        for kh in range(KH):
            at = 8 * (KH * f + kh)
            width = min(128, NLON_MAX - 128 * kh)
            tile = jnp.where(lon + 128 * kh < cycles, lat[at:at + 8, :], 0.0).astype(BF16)
            out_ref[f, :, 128 * kh:128 * kh + width] = tile[:, 0:width]

    def all_sent(block, count, sem):
        part = block.at[pl.ds(0, count)]
        pltpu.make_async_copy(part, part, sem).wait()

    all_sent(recv_s, LEVS - 1, ss_send)

    @pl.when(c == half)
    def _():
        all_sent(recv_l, CHIPS - 1, sl_send)

    @pl.when(c != half)
    def _():
        all_sent(recv_l, CHIPS, sl_send)

    all_sent(recv_x, LEVS - 1, sx_send)
    all_sent(recv_z, WAVES - 1, sz_send)


def on_device(spec, legendre, mids, band_lats, nlon):
    spec_rows = spec.reshape(240, MW)
    tables = jnp.transpose(legendre, (0, 2, 1))
    hbm = pl.BlockSpec(memory_space=pltpu.HBM)
    vmem = pl.BlockSpec(memory_space=pltpu.VMEM)
    dma = pltpu.SemaphoreType.DMA
    planes = pl.pallas_call(
        kernel,
        out_shape=jax.ShapeDtypeStruct((3, LAT_MAX, NLON_MAX), BF16),
        in_specs=[hbm] * 6,
        out_specs=vmem,
        scratch_shapes=[
            pltpu.SMEM((MW,), jnp.int32),
            pltpu.SMEM((WAVES,), jnp.int32),
            pltpu.SMEM((PAIRS,), jnp.int32),
            pltpu.VMEM((240, MW), BF16),
            pltpu.VMEM((SLOTS, PAIRS, BLOCK), BF16),
            pltpu.VMEM((16, 128), jnp.int32),
            pltpu.VMEM((1, MW), F32),
            pltpu.VMEM((10, 256, 128), F32),
            pltpu.VMEM((CHIPS, 2, 32, HALF), BF16),
            pltpu.VMEM((CHIPS, LEG_ROWS, 128), BF16),
            pltpu.VMEM((LEVS, 32, HALF), BF16),
            pltpu.VMEM((8, LEG_ROWS, 128), BF16),
            pltpu.VMEM((HALF, 256), BF16),
            pltpu.VMEM((512, 256), F32),
            pltpu.VMEM((LEVS, 32, 256), BF16),
            pltpu.VMEM((LEVS, 32, 256), BF16),
            pltpu.VMEM((256, 256), BF16),
            pltpu.VMEM((WAVES, 16, 128), BF16),
            pltpu.VMEM((WAVES, 16, 128), BF16),
            pltpu.VMEM((512, 128), F32),
            pltpu.VMEM((512, 128), BF16),
            pltpu.VMEM((20, 128, 256), BF16),
            pltpu.VMEM((MW, 128), F32),
            pltpu.VMEM((LAT_MAX, MW, 128), F32),
            pltpu.VMEM((LAT_MAX, MW, 128), F32),
            pltpu.VMEM((LAT_MAX, 128, 2 * MW), BF16),
            pltpu.VMEM((LAT_MAX, 2 * MW, 128), BF16),
            pltpu.VMEM((1024, 128), F32),
            dma((6,)), dma, dma, dma, dma, dma, dma, dma, dma,
        ],
        compiler_params=pltpu.CompilerParams(
            collective_id=0, has_side_effects=True, vmem_limit_bytes=58 * 2**20
        ),
    )(mids, band_lats, nlon, spec_rows, tables, mids.reshape(10, 128))
    return jnp.transpose(planes, (1, 0, 2)).reshape(LAT_MAX, 3, 1, NLON_MAX)


def solution(mesh):
    in_specs = (P(None, None, "lev", "wave", None), P("wave", "lev", None), P(), P(), P())
    out_specs = P("wave", None, "lev", None)
    return jax.shard_map(
        on_device, mesh=mesh, in_specs=in_specs, out_specs=out_specs, check_vma=False
    )
```

```python
import jax
import jax.numpy as jnp
from jax import lax
from jax.experimental import pallas as pl
from jax.experimental.pallas import tpu as pltpu
from jax.sharding import PartitionSpec as P

LAT_MAX = 8
NLON_MAX = 5136
KH = 41
WAVES = 32
LEVS = 16
CHIPS = 8
SLOTS = 40
GROUP = 5
MW = 1280
HALF = 640
BLOCK = 80
LEG_ROWS = 208
PAIRS = 64
LATS = 128
TWO_PI = 6.283185307179586
F32 = jnp.float32
BF16 = jnp.bfloat16
MESH = pl.DeviceIdType.MESH

SIN = []
_term = TWO_PI
for _i in range(6):
    SIN.append(_term)
    _term = -_term * TWO_PI * TWO_PI / ((2 * _i + 2) * (2 * _i + 3))


def quarter_sine(y):
    y2 = y * y
    acc = jnp.full_like(y2, SIN[-1])
    for c in SIN[-2::-1]:
        acc = acc * y2 + c
    return acc * y


def cos_sin(steps, cycle, inverse):
    rest = steps - jnp.floor(steps * inverse + 0.5) * cycle
    t = rest * inverse
    a = jnp.abs(t)
    folded = jnp.where(a > 0.25, jnp.where(t < 0, -0.5, 0.5) - t, t)
    return quarter_sine(0.25 - a), quarter_sine(folded)


def nt_dot(a, b):
    return lax.dot_general(a, b, (((1,), (1,)), ((), ())), preferred_element_type=F32)


def kernel(
    mids_hbm, bands_hbm, nlon_hbm, spec_hbm, leg_hbm, mids_rows_hbm, out_ref,
    mids_ref, bands_ref, nlon_ref, spec_ref, leg_ref, mids_rows, mrow_ref, spec_f, send_s, send_l, recv_s, recv_l, rhs, sums, send_r, recv_x,
    onehot, send_y, recv_z, zf, zs, expand, mcol, cosc, sinc, tw, mod, lat,
    load_sem, ss_send, ss_recv, sl_send, sl_recv, sx_send, sx_recv, sz_send, sz_recv,
):
    w = lax.axis_index("wave")
    me = lax.axis_index("lev")
    z = me // 2
    c = me - 2 * z
    half = z // 4

    barrier = pltpu.get_barrier_semaphore()
    for k in range(1, LEVS):
        pl.semaphore_signal(barrier, inc=1, device_id={"lev": lax.rem(me + k, LEVS)}, device_id_type=MESH)
    for k in range(1, WAVES):
        pl.semaphore_signal(barrier, inc=1, device_id={"wave": lax.rem(w + k, WAVES)}, device_id_type=MESH)

    mids_rows[...] = jnp.zeros_like(mids_rows)
    loads = [
        pltpu.make_async_copy(spec_hbm, spec_ref, load_sem.at[0]),
        pltpu.make_async_copy(leg_hbm, leg_ref, load_sem.at[1]),
        pltpu.make_async_copy(mids_rows_hbm, mids_rows.at[0:10], load_sem.at[2]),
        pltpu.make_async_copy(mids_hbm, mids_ref, load_sem.at[3]),
        pltpu.make_async_copy(bands_hbm, bands_ref, load_sem.at[4]),
        pltpu.make_async_copy(nlon_hbm, nlon_ref, load_sem.at[5]),
    ]
    for load in loads:
        load.start()
    loads[0].wait()

    for tile in range(10):
        spec_f[tile, 0:240, :] = spec_ref[:, 128 * tile:128 * tile + 128].astype(F32)
        spec_f[tile, 240:256, :] = jnp.zeros((16, 128), F32)

    unit = jnp.where(
        lax.broadcasted_iota(jnp.int32, (BLOCK, BLOCK), 0) == lax.broadcasted_iota(jnp.int32, (BLOCK, BLOCK), 1),
        1.0, 0.0,
    ).astype(BF16)

    fold = jnp.where(
        (lax.broadcasted_iota(jnp.int32, (48, BLOCK), 0) == lax.broadcasted_iota(jnp.int32, (48, BLOCK), 1))
        | (lax.broadcasted_iota(jnp.int32, (48, BLOCK), 0) + 40 == lax.broadcasted_iota(jnp.int32, (48, BLOCK), 1)),
        1.0, 0.0,
    )
    fold = jnp.where(lax.broadcasted_iota(jnp.int32, (48, BLOCK), 0) < 40, fold, 0.0).astype(BF16)
    upper = (lax.broadcasted_iota(jnp.int32, (LATS, BLOCK), 0) < PAIRS) == (
        lax.broadcasted_iota(jnp.int32, (LATS, BLOCK), 1) < 40
    )
    loads[1].wait()
    pl.semaphore_wait(barrier, LEVS + WAVES - 2)

    def spec_copy(k, h):
        to = lax.rem(z + k, CHIPS)
        return pltpu.make_async_remote_copy(
            src_ref=send_s.at[to, h], dst_ref=recv_s.at[me], send_sem=ss_send,
            recv_sem=ss_recv, device_id={"lev": 2 * to + h}, device_id_type=MESH,
        )

    def leg_copy(k):
        to = lax.rem(z + k, CHIPS)
        return pltpu.make_async_remote_copy(
            src_ref=send_l.at[to], dst_ref=recv_l.at[lax.rem(me, 8)], send_sem=sl_send,
            recv_sem=sl_recv, device_id={"lev": 2 * to + half}, device_id_type=MESH,
        )

    def prepare(k):
        to = lax.rem(z + k, CHIPS)
        for tile in range(10):
            rows = spec_f[tile, pl.ds(to, 32, stride=8), :].astype(BF16)
            send_s[to, tile // 5, :, 128 * (tile % 5):128 * (tile % 5) + 128] = rows
        for p in range(2):
            stacked = jnp.concatenate([leg_ref[16 * p + to], leg_ref[16 * p + 8 + to]], axis=0)
            send_l[to, BLOCK * p:BLOCK * p + BLOCK, :] = nt_dot(unit, stacked).astype(BF16)
        last = leg_ref[32 + to].astype(F32)
        stacked = jnp.where(upper, jnp.concatenate([last, last], axis=0), 0.0).astype(BF16)
        send_l[to, 2 * BLOCK:LEG_ROWS, :] = nt_dot(fold, stacked).astype(BF16)

    def send_far(i, carry):
        k = jnp.where(lax.rem(i, 2) == 1, 4 - (i + 1) // 2, 4 + i // 2)
        prepare(k)
        for h in range(2):
            spec_copy(k, h).start()
        leg_copy(k).start()
        return carry

    lax.fori_loop(0, CHIPS - 1, send_far, 0)
    prepare(0)
    for h in range(2):
        @pl.when(c == h)
        def _():
            pltpu.make_async_copy(send_s.at[z, h], recv_s.at[me], ss_recv).start()

        @pl.when(c != h)
        def _():
            spec_copy(0, h).start()

    @pl.when(c == half)
    def _():
        pltpu.make_async_copy(send_l.at[z], recv_l.at[lax.rem(me, 8)], sl_recv).start()

    @pl.when(c != half)
    def _():
        leg_copy(0).start()

    for load in loads[2:]:
        load.wait()

    start = jnp.int32(0)
    own_start = jnp.int32(0)
    sub16 = lax.broadcasted_iota(jnp.int32, (16, 128), 0)
    lane = lax.broadcasted_iota(jnp.int32, (16, 128), 1)
    lat_of = jnp.where(lane < PAIRS, lane, LATS - 1 - (lane - PAIRS))
    for e in range(WAVES // 2):
        count_a, count_b = bands_ref[2 * e], bands_ref[2 * e + 1]
        start_b = start + count_a
        own_start = jnp.where(w == 2 * e, start, jnp.where(w == 2 * e + 1, start_b, own_start))
        inner = sub16 & 7
        wanted = jnp.where(sub16 < 8, start, start_b) + inner
        filled = inner < jnp.where(sub16 < 8, count_a, count_b)
        match = jnp.where(filled, wanted, -1) == lat_of
        onehot[16 * e:16 * e + 16, :] = jnp.where(match, 1.0, 0.0).astype(BF16)
        start = start_b + count_b

    def cycle_of(slot):
        latitude = jnp.minimum(own_start + slot, LATS - 1)
        pair = jnp.where(latitude < PAIRS, latitude, LATS - 1 - latitude)
        return nlon_ref[pair]

    krow = lax.broadcasted_iota(jnp.int32, (128, 256), 0)
    klane = lax.broadcasted_iota(jnp.int32, (128, 256), 1)
    col = klane & 127
    channel = jnp.where(col >= KH, 1, 0) + jnp.where(col >= 2 * KH, 1, 0) + jnp.where(col >= 3 * KH, 100, 0)
    base = krow - (GROUP * channel + jnp.where(klane >= 128, 15, 0))

    def fill_expand(i, carry):
        zl = i // GROUP
        match = base == zl * 32 + (i - GROUP * zl)
        expand[i] = jnp.where(match, 1.0, 0.0).astype(BF16)
        return carry

    lax.fori_loop(0, 20, fill_expand, 0)

    natural = mids_rows[...].astype(F32)
    high = jnp.floor(natural * 0.125)
    digits = jnp.concatenate([high, natural - 8.0 * high], axis=0).astype(BF16)
    for t in range(10):
        place = lax.broadcasted_iota(jnp.int32, (128, 128), 1) + 128 * t
        group = place >> 6
        zl = jnp.where(group >= 5, 1, 0) + jnp.where(group >= 10, 1, 0) + jnp.where(group >= 15, 1, 0)
        source = SLOTS * ((place & 63) >> 1) + 8 * (group - GROUP * zl) + 4 * (place & 1) + zl
        pick = lax.broadcasted_iota(jnp.int32, (128, 128), 0) == (source & 127)
        found = jnp.dot(digits, jnp.where(pick, 1.0, 0.0).astype(BF16), preferred_element_type=F32)
        found = 8.0 * found[0:16, :] + found[16:32, :]
        here = lax.broadcasted_iota(jnp.int32, (16, 128), 0) == (source[0:16, :] >> 7)
        row = jnp.sum(jnp.where(here, found, 0.0), axis=0, keepdims=True)
        mrow_ref[0:1, 128 * t:128 * t + 128] = row
        mcol[128 * t:128 * t + 128, :] = jnp.broadcast_to(row, (128, 128)).T

    col1 = lax.broadcasted_iota(jnp.int32, (1, 128), 1)
    channel1 = jnp.where(col1 >= KH, 1, 0) + jnp.where(col1 >= 2 * KH, 1, 0)
    coarse_steps = (128 * (col1 - KH * channel1)).astype(F32)
    a_steps = (16 * lax.broadcasted_iota(jnp.int32, (8, 128), 0)).astype(F32)
    b_steps = lax.broadcasted_iota(jnp.int32, (16, 128), 0).astype(F32)

    def tables(slot, carry):
        cycle = jnp.full((1, 128), cycle_of(slot), jnp.int32).astype(F32)
        inverse = 1.0 / cycle

        def coarse(i, inner_carry):
            at = pl.multiple_of(128 * i, 128)
            cos_part, sin_part = cos_sin(mcol[pl.ds(at, 128), :] * coarse_steps, cycle, inverse)
            cosc[slot, pl.ds(at, 128), :] = cos_part
            sinc[slot, pl.ds(at, 128), :] = sin_part
            return inner_carry

        lax.fori_loop(0, 10, coarse, 0)

        def fine(i, inner_carry):
            at = pl.multiple_of(128 * i, 128)
            m = mrow_ref[0:1, pl.ds(at, 128)]
            weight = jnp.where(m == 0, 1.0, 2.0)
            weight = jnp.where(2 * m < cycle, weight, 0.0)
            cos_a, sin_a = cos_sin(m * a_steps, cycle, inverse)
            cos_b, sin_b = cos_sin(m * b_steps, cycle, inverse)
            cos_a = cos_a * weight
            sin_a = sin_a * weight
            for a in range(8):
                ca, sa = cos_a[a:a + 1, :], sin_a[a:a + 1, :]
                tw[slot, 16 * a:16 * a + 16, pl.ds(at, 128)] = (ca * cos_b - sa * sin_b).astype(BF16)
                other = pl.multiple_of(at + MW, 128)
                tw[slot, 16 * a:16 * a + 16, pl.ds(other, 128)] = (-(sa * cos_b + ca * sin_b)).astype(BF16)
            return inner_carry

        lax.fori_loop(0, 10, fine, 0)
        return carry

    lax.fori_loop(0, LAT_MAX, tables, 0)

    pltpu.make_async_copy(recv_s, recv_s, ss_recv).wait()
    pltpu.make_async_copy(recv_l, recv_l, sl_recv).wait()

    left = recv_s[...].reshape(512, HALF)
    row_r = lax.broadcasted_iota(jnp.int32, (512, 256), 0) & 31
    j_r = row_r - GROUP * jnp.floor((row_r.astype(F32) + 0.5) * 0.2).astype(jnp.int32)
    lane_r = lax.broadcasted_iota(jnp.int32, (512, 256), 1)
    degree = lax.broadcasted_iota(jnp.int32, (HALF, 128), 0) + HALF * c
    lane_n = lax.broadcasted_iota(jnp.int32, (HALF, 128), 1)
    for p in range(3):
        m_a = mids_ref[SLOTS * w + 16 * p + z]
        m_b = mids_ref[SLOTS * w + 16 * p + 8 + z] if p < 2 else m_a
        m = jnp.where(lane_n < PAIRS, m_a, m_b)
        if p < 2:
            table = recv_l[:, BLOCK * p:BLOCK * p + BLOCK, :].astype(F32).reshape(HALF, 128)
        else:
            packed = recv_l[:, 2 * BLOCK:LEG_ROWS, :].astype(F32)
            swapped = jnp.concatenate([packed[:, :, 64:128], packed[:, :, 0:64]], axis=2)
            table = jnp.concatenate([packed[:, 0:40], swapped[:, 0:40]], axis=1).reshape(HALF, 128)
        table = jnp.where(degree >= m, table, 0.0)
        rhs[:, 0:128] = table.astype(BF16)
        rhs[:, 128:256] = jnp.where(((degree + m) & 1) == 1, -table, table).astype(BF16)
        terms = jnp.dot(left, rhs[...], preferred_element_type=F32)
        if p == 0:
            sums[...] = terms
        else:
            sums[...] = jnp.where(j_r >= 2 * p, terms, sums[...])
    north, south = sums[:, 0:128], sums[:, 128:256]
    odd = (j_r[:, 0:128] & 1) == 1
    north = jnp.where(odd, pltpu.roll(north, PAIRS, 1), north)
    south = jnp.where(odd, south, pltpu.roll(south, PAIRS, 1))
    both_halves = jnp.where(lane_r[:, 0:128] < PAIRS, north, south)
    send_r[...] = both_halves.astype(BF16).reshape(LEVS, 32, 128)

    def level_copy(k):
        to = lax.rem(me + k, LEVS)
        return pltpu.make_async_remote_copy(
            src_ref=send_r.at[to], dst_ref=recv_x.at[me], send_sem=sx_send,
            recv_sem=sx_recv, device_id={"lev": to}, device_id_type=MESH,
        )

    for k in sorted(range(1, LEVS), key=lambda k: abs(k - LEVS // 2)):
        level_copy(k).start()
    pltpu.make_async_copy(send_r.at[me], recv_x.at[me], sx_recv).start()
    pltpu.make_async_copy(recv_x, recv_x, sx_recv).wait()

    got = recv_x[...].astype(F32).reshape(CHIPS, 2, 32, 128)
    level_sums = (got[:, 0] + got[:, 1]).reshape(256, 128).astype(BF16)
    by_slot = nt_dot(onehot[...], level_sums)
    low = by_slot[:, 0:128].reshape(WAVES, 8, 128)
    high = by_slot[:, 128:256].reshape(WAVES, 8, 128)
    send_y[...] = jnp.concatenate([low, high], axis=1).astype(BF16)

    def band_copy(k):
        to = lax.rem(w + k, WAVES)
        return pltpu.make_async_remote_copy(
            src_ref=send_y.at[to], dst_ref=recv_z.at[w], send_sem=sz_send,
            recv_sem=sz_recv, device_id={"wave": to}, device_id_type=MESH,
        )

    for k in sorted(range(1, WAVES), key=lambda k: abs(k - WAVES // 2)):
        band_copy(k).start()
    pltpu.make_async_copy(send_y.at[w], recv_z.at[w], sz_recv).start()
    pltpu.make_async_copy(recv_z, recv_z, sz_recv).wait()

    zf[...] = recv_z[...].astype(F32).reshape(512, 128)
    for slot in range(LAT_MAX):
        zs[64 * slot:64 * slot + 64, :] = zf[pl.ds(slot, 64, stride=8), :].astype(BF16)

    def modulate(i, carry):
        both = jnp.dot(zs[...], expand[i], preferred_element_type=F32)
        at = pl.multiple_of(64 * i, 64)
        other = pl.multiple_of(64 * i + MW, 64)
        for slot in range(LAT_MAX):
            re = both[64 * slot:64 * slot + 64, 0:128]
            im = both[64 * slot:64 * slot + 64, 128:256]
            cos_part = cosc[slot, pl.ds(at, 64), :]
            sin_part = sinc[slot, pl.ds(at, 64), :]
            mod[slot, pl.ds(at, 64), :] = (re * cos_part - im * sin_part).astype(BF16)
            mod[slot, pl.ds(other, 64), :] = (re * sin_part + im * cos_part).astype(BF16)
        return carry

    lax.fori_loop(0, 20, modulate, 0)

    def transform(slot, carry):
        points = jnp.dot(tw[slot], mod[slot], preferred_element_type=F32)
        lat[pl.ds(slot, 128, stride=8), :] = points.T
        return carry

    lax.fori_loop(0, LAT_MAX, transform, 0)

    slot_of = lax.broadcasted_iota(jnp.int32, (8, 128), 0)
    lon = lax.broadcasted_iota(jnp.int32, (8, 128), 1)
    cycles = jnp.zeros((8, 128), jnp.int32)
    for slot in range(LAT_MAX):
        cycles = jnp.where(slot_of == slot, cycle_of(slot), cycles)
    for f in range(3):
        for kh in range(KH):
            at = 8 * (KH * f + kh)
            width = min(128, NLON_MAX - 128 * kh)
            tile = jnp.where(lon + 128 * kh < cycles, lat[at:at + 8, :], 0.0).astype(BF16)
            out_ref[f, :, 128 * kh:128 * kh + width] = tile[:, 0:width]

    def all_sent(block, count, sem):
        part = block.at[pl.ds(0, count)]
        pltpu.make_async_copy(part, part, sem).wait()

    all_sent(recv_s, LEVS - 1, ss_send)

    @pl.when(c == half)
    def _():
        all_sent(recv_l, CHIPS - 1, sl_send)

    @pl.when(c != half)
    def _():
        all_sent(recv_l, CHIPS, sl_send)

    all_sent(recv_x, LEVS - 1, sx_send)
    all_sent(recv_z, WAVES - 1, sz_send)


def on_device(spec, legendre, mids, band_lats, nlon):
    spec_rows = spec.reshape(240, MW)
    tables = jnp.transpose(legendre, (0, 2, 1))
    hbm = pl.BlockSpec(memory_space=pltpu.HBM)
    vmem = pl.BlockSpec(memory_space=pltpu.VMEM)
    dma = pltpu.SemaphoreType.DMA
    planes = pl.pallas_call(
        kernel,
        out_shape=jax.ShapeDtypeStruct((3, LAT_MAX, NLON_MAX), BF16),
        in_specs=[hbm] * 6,
        out_specs=vmem,
        scratch_shapes=[
            pltpu.SMEM((MW,), jnp.int32),
            pltpu.SMEM((WAVES,), jnp.int32),
            pltpu.SMEM((PAIRS,), jnp.int32),
            pltpu.VMEM((240, MW), BF16),
            pltpu.VMEM((SLOTS, PAIRS, BLOCK), BF16),
            pltpu.VMEM((16, 128), jnp.int32),
            pltpu.VMEM((1, MW), F32),
            pltpu.VMEM((10, 256, 128), F32),
            pltpu.VMEM((CHIPS, 2, 32, HALF), BF16),
            pltpu.VMEM((CHIPS, LEG_ROWS, 128), BF16),
            pltpu.VMEM((LEVS, 32, HALF), BF16),
            pltpu.VMEM((8, LEG_ROWS, 128), BF16),
            pltpu.VMEM((HALF, 256), BF16),
            pltpu.VMEM((512, 256), F32),
            pltpu.VMEM((LEVS, 32, 128), BF16),
            pltpu.VMEM((LEVS, 32, 128), BF16),
            pltpu.VMEM((256, 128), BF16),
            pltpu.VMEM((WAVES, 16, 128), BF16),
            pltpu.VMEM((WAVES, 16, 128), BF16),
            pltpu.VMEM((512, 128), F32),
            pltpu.VMEM((512, 128), BF16),
            pltpu.VMEM((20, 128, 256), BF16),
            pltpu.VMEM((MW, 128), F32),
            pltpu.VMEM((LAT_MAX, MW, 128), F32),
            pltpu.VMEM((LAT_MAX, MW, 128), F32),
            pltpu.VMEM((LAT_MAX, 128, 2 * MW), BF16),
            pltpu.VMEM((LAT_MAX, 2 * MW, 128), BF16),
            pltpu.VMEM((1024, 128), F32),
            dma((6,)), dma, dma, dma, dma, dma, dma, dma, dma,
        ],
        compiler_params=pltpu.CompilerParams(
            collective_id=0, has_side_effects=True, vmem_limit_bytes=58 * 2**20
        ),
    )(mids, band_lats, nlon, spec_rows, tables, mids.reshape(10, 128))
    return jnp.transpose(planes, (1, 0, 2)).reshape(LAT_MAX, 3, 1, NLON_MAX)


def solution(mesh):
    in_specs = (P(None, None, "lev", "wave", None), P("wave", "lev", None), P(), P(), P())
    out_specs = P("wave", None, "lev", None)
    return jax.shard_map(
        on_device, mesh=mesh, in_specs=in_specs, out_specs=out_specs, check_vma=False
    )
```

```python
import jax
import jax.numpy as jnp
from jax import lax
from jax.experimental import pallas as pl
from jax.experimental.pallas import tpu as pltpu
from jax.sharding import PartitionSpec as P

LAT_MAX = 8
NLON_MAX = 5136
KH = 41
WAVES = 32
LEVS = 16
CHIPS = 8
SLOTS = 40
GROUP = 5
MW = 1280
HALF = 640
BLOCK = 80
LEG_ROWS = 208
PAIRS = 64
LATS = 128
TWO_PI = 6.283185307179586
F32 = jnp.float32
BF16 = jnp.bfloat16
MESH = pl.DeviceIdType.MESH

SIN = []
_term = TWO_PI
for _i in range(6):
    SIN.append(_term)
    _term = -_term * TWO_PI * TWO_PI / ((2 * _i + 2) * (2 * _i + 3))


def quarter_sine(y):
    y2 = y * y
    acc = jnp.full_like(y2, SIN[-1])
    for c in SIN[-2::-1]:
        acc = acc * y2 + c
    return acc * y


def cos_sin(steps, cycle, inverse):
    rest = steps - jnp.floor(steps * inverse + 0.5) * cycle
    t = rest * inverse
    a = jnp.abs(t)
    folded = jnp.where(a > 0.25, jnp.where(t < 0, -0.5, 0.5) - t, t)
    return quarter_sine(0.25 - a), quarter_sine(folded)


def nt_dot(a, b):
    return lax.dot_general(a, b, (((1,), (1,)), ((), ())), preferred_element_type=F32)


def kernel(
    mids_hbm, bands_hbm, nlon_hbm, spec_hbm, leg_hbm, mids_rows_hbm, out_ref,
    mids_ref, bands_ref, nlon_ref, spec_ref, leg_ref, mids_rows, mrow_ref, spec_f, send_s, send_l, recv_s, recv_l, rhs, slot_j, send_r, recv_x,
    onehot, send_y, recv_z, zf, zs, expand, mcol, cosc, sinc, tw, mod, lat,
    load_sem, ss_send, ss_recv, sl_send, sl_recv, sx_send, sx_recv, sz_send, sz_recv,
):
    w = lax.axis_index("wave")
    me = lax.axis_index("lev")
    z = me // 2
    c = me - 2 * z
    half = z // 4

    mids_rows[...] = jnp.zeros_like(mids_rows)
    loads = [
        pltpu.make_async_copy(leg_hbm, leg_ref, load_sem.at[0]),
        pltpu.make_async_copy(spec_hbm, spec_ref, load_sem.at[1]),
        pltpu.make_async_copy(mids_rows_hbm, mids_rows.at[0:10], load_sem.at[2]),
        pltpu.make_async_copy(mids_hbm, mids_ref, load_sem.at[3]),
        pltpu.make_async_copy(bands_hbm, bands_ref, load_sem.at[4]),
        pltpu.make_async_copy(nlon_hbm, nlon_ref, load_sem.at[5]),
    ]
    for load in loads:
        load.start()

    barrier = pltpu.get_barrier_semaphore()
    for k in range(1, LEVS):
        pl.semaphore_signal(barrier, inc=1, device_id={"lev": lax.rem(me + k, LEVS)}, device_id_type=MESH)
    for k in range(1, WAVES):
        pl.semaphore_signal(barrier, inc=1, device_id={"wave": lax.rem(w + k, WAVES)}, device_id_type=MESH)


    unit = jnp.where(
        lax.broadcasted_iota(jnp.int32, (BLOCK, BLOCK), 0) == lax.broadcasted_iota(jnp.int32, (BLOCK, BLOCK), 1),
        1.0, 0.0,
    ).astype(BF16)

    fold = jnp.where(
        (lax.broadcasted_iota(jnp.int32, (48, BLOCK), 0) == lax.broadcasted_iota(jnp.int32, (48, BLOCK), 1))
        | (lax.broadcasted_iota(jnp.int32, (48, BLOCK), 0) + 40 == lax.broadcasted_iota(jnp.int32, (48, BLOCK), 1)),
        1.0, 0.0,
    )
    fold = jnp.where(lax.broadcasted_iota(jnp.int32, (48, BLOCK), 0) < 40, fold, 0.0).astype(BF16)
    upper = (lax.broadcasted_iota(jnp.int32, (LATS, BLOCK), 0) < PAIRS) == (
        lax.broadcasted_iota(jnp.int32, (LATS, BLOCK), 1) < 40
    )
    loads[0].wait()
    pl.semaphore_wait(barrier, LEVS + WAVES - 2)

    def spec_copy(k, h):
        to = lax.rem(z + k, CHIPS)
        return pltpu.make_async_remote_copy(
            src_ref=send_s.at[to, h], dst_ref=recv_s.at[me], send_sem=ss_send,
            recv_sem=ss_recv, device_id={"lev": 2 * to + h}, device_id_type=MESH,
        )

    def leg_copy(k):
        to = lax.rem(z + k, CHIPS)
        return pltpu.make_async_remote_copy(
            src_ref=send_l.at[to], dst_ref=recv_l.at[lax.rem(me, 8)], send_sem=sl_send,
            recv_sem=sl_recv, device_id={"lev": 2 * to + half}, device_id_type=MESH,
        )

    def order_of(i):
        return jnp.where(lax.rem(i, 2) == 1, 4 - (i + 1) // 2, 4 + i // 2)

    def prepare_leg(k):
        to = lax.rem(z + k, CHIPS)
        for p in range(2):
            stacked = jnp.concatenate([leg_ref[16 * p + to], leg_ref[16 * p + 8 + to]], axis=0)
            send_l[to, BLOCK * p:BLOCK * p + BLOCK, :] = nt_dot(unit, stacked).astype(BF16)
        last = leg_ref[32 + to].astype(F32)
        stacked = jnp.where(upper, jnp.concatenate([last, last], axis=0), 0.0).astype(BF16)
        send_l[to, 2 * BLOCK:LEG_ROWS, :] = nt_dot(fold, stacked).astype(BF16)

    def prepare_spec(k):
        to = lax.rem(z + k, CHIPS)
        for tile in range(10):
            rows = spec_f[tile, pl.ds(to, 32, stride=8), :].astype(BF16)
            send_s[to, tile // 5, :, 128 * (tile % 5):128 * (tile % 5) + 128] = rows

    def send_leg(i, carry):
        k = order_of(i)
        prepare_leg(k)
        leg_copy(k).start()
        return carry

    lax.fori_loop(0, CHIPS - 1, send_leg, 0)
    prepare_leg(0)

    @pl.when(c == half)
    def _():
        pltpu.make_async_copy(send_l.at[z], recv_l.at[lax.rem(me, 8)], sl_recv).start()

    @pl.when(c != half)
    def _():
        leg_copy(0).start()

    loads[1].wait()
    for tile in range(10):
        spec_f[tile, 0:240, :] = spec_ref[:, 128 * tile:128 * tile + 128].astype(F32)
        spec_f[tile, 240:256, :] = jnp.zeros((16, 128), F32)

    def send_spec(i, carry):
        k = order_of(i)
        prepare_spec(k)
        for h in range(2):
            spec_copy(k, h).start()
        return carry

    lax.fori_loop(0, CHIPS - 1, send_spec, 0)
    prepare_spec(0)
    for h in range(2):
        @pl.when(c == h)
        def _():
            pltpu.make_async_copy(send_s.at[z, h], recv_s.at[me], ss_recv).start()

        @pl.when(c != h)
        def _():
            spec_copy(0, h).start()

    for load in loads[2:]:
        load.wait()

    start = jnp.int32(0)
    own_start = jnp.int32(0)
    sub16 = lax.broadcasted_iota(jnp.int32, (16, 128), 0)
    lane = lax.broadcasted_iota(jnp.int32, (16, 128), 1)
    lat_of = jnp.where(lane < PAIRS, lane, LATS - 1 - (lane - PAIRS))
    for e in range(WAVES // 2):
        count_a, count_b = bands_ref[2 * e], bands_ref[2 * e + 1]
        start_b = start + count_a
        own_start = jnp.where(w == 2 * e, start, jnp.where(w == 2 * e + 1, start_b, own_start))
        inner = sub16 & 7
        wanted = jnp.where(sub16 < 8, start, start_b) + inner
        filled = inner < jnp.where(sub16 < 8, count_a, count_b)
        match = jnp.where(filled, wanted, -1) == lat_of
        onehot[16 * e:16 * e + 16, :] = jnp.where(match, 1.0, 0.0).astype(BF16)
        start = start_b + count_b

    def cycle_of(slot):
        latitude = jnp.minimum(own_start + slot, LATS - 1)
        pair = jnp.where(latitude < PAIRS, latitude, LATS - 1 - latitude)
        return nlon_ref[pair]

    krow = lax.broadcasted_iota(jnp.int32, (128, 256), 0)
    klane = lax.broadcasted_iota(jnp.int32, (128, 256), 1)
    col = klane & 127
    channel = jnp.where(col >= KH, 1, 0) + jnp.where(col >= 2 * KH, 1, 0) + jnp.where(col >= 3 * KH, 100, 0)
    base = krow - (GROUP * channel + jnp.where(klane >= 128, 15, 0))

    def fill_expand(i, carry):
        zl = i // GROUP
        match = base == zl * 32 + (i - GROUP * zl)
        expand[i] = jnp.where(match, 1.0, 0.0).astype(BF16)
        return carry

    lax.fori_loop(0, 20, fill_expand, 0)

    natural = mids_rows[...].astype(F32)
    high = jnp.floor(natural * 0.125)
    digits = jnp.concatenate([high, natural - 8.0 * high], axis=0).astype(BF16)
    for t in range(10):
        place = lax.broadcasted_iota(jnp.int32, (128, 128), 1) + 128 * t
        group = place >> 6
        zl = jnp.where(group >= 5, 1, 0) + jnp.where(group >= 10, 1, 0) + jnp.where(group >= 15, 1, 0)
        source = SLOTS * ((place & 63) >> 1) + 8 * (group - GROUP * zl) + 4 * (place & 1) + zl
        pick = lax.broadcasted_iota(jnp.int32, (128, 128), 0) == (source & 127)
        found = jnp.dot(digits, jnp.where(pick, 1.0, 0.0).astype(BF16), preferred_element_type=F32)
        found = 8.0 * found[0:16, :] + found[16:32, :]
        here = lax.broadcasted_iota(jnp.int32, (16, 128), 0) == (source[0:16, :] >> 7)
        row = jnp.sum(jnp.where(here, found, 0.0), axis=0, keepdims=True)
        mrow_ref[0:1, 128 * t:128 * t + 128] = row
        mcol[128 * t:128 * t + 128, :] = jnp.broadcast_to(row, (128, 128)).T

    col1 = lax.broadcasted_iota(jnp.int32, (1, 128), 1)
    channel1 = jnp.where(col1 >= KH, 1, 0) + jnp.where(col1 >= 2 * KH, 1, 0)
    coarse_steps = (128 * (col1 - KH * channel1)).astype(F32)
    a_steps = (16 * lax.broadcasted_iota(jnp.int32, (8, 128), 0)).astype(F32)
    b_steps = lax.broadcasted_iota(jnp.int32, (16, 128), 0).astype(F32)

    def tables(slot, carry):
        cycle = jnp.full((1, 128), cycle_of(slot), jnp.int32).astype(F32)
        inverse = 1.0 / cycle

        def coarse(i, inner_carry):
            at = pl.multiple_of(128 * i, 128)
            cos_part, sin_part = cos_sin(mcol[pl.ds(at, 128), :] * coarse_steps, cycle, inverse)
            cosc[slot, pl.ds(at, 128), :] = cos_part
            sinc[slot, pl.ds(at, 128), :] = sin_part
            return inner_carry

        lax.fori_loop(0, 10, coarse, 0)

        def fine(i, inner_carry):
            at = pl.multiple_of(128 * i, 128)
            m = mrow_ref[0:1, pl.ds(at, 128)]
            weight = jnp.where(m == 0, 1.0, 2.0)
            weight = jnp.where(2 * m < cycle, weight, 0.0)
            cos_a, sin_a = cos_sin(m * a_steps, cycle, inverse)
            cos_b, sin_b = cos_sin(m * b_steps, cycle, inverse)
            cos_a = cos_a * weight
            sin_a = sin_a * weight
            for a in range(8):
                ca, sa = cos_a[a:a + 1, :], sin_a[a:a + 1, :]
                tw[slot, 16 * a:16 * a + 16, pl.ds(at, 128)] = (ca * cos_b - sa * sin_b).astype(BF16)
                other = pl.multiple_of(at + MW, 128)
                tw[slot, 16 * a:16 * a + 16, pl.ds(other, 128)] = (-(sa * cos_b + ca * sin_b)).astype(BF16)
            return inner_carry

        lax.fori_loop(0, 10, fine, 0)
        return carry

    lax.fori_loop(0, LAT_MAX, tables, 0)

    pltpu.make_async_copy(recv_l, recv_l, sl_recv).wait()
    degree = lax.broadcasted_iota(jnp.int32, (HALF, 128), 0) + HALF * c
    lane_n = lax.broadcasted_iota(jnp.int32, (HALF, 128), 1)
    for p in range(3):
        m_a = mids_ref[SLOTS * w + 16 * p + z]
        m_b = mids_ref[SLOTS * w + 16 * p + 8 + z] if p < 2 else m_a
        m = jnp.where(lane_n < PAIRS, m_a, m_b)
        if p < 2:
            table = recv_l[:, BLOCK * p:BLOCK * p + BLOCK, :].astype(F32).reshape(HALF, 128)
        else:
            packed = recv_l[:, 2 * BLOCK:LEG_ROWS, :].astype(F32)
            swapped = jnp.concatenate([packed[:, :, 64:128], packed[:, :, 0:64]], axis=2)
            table = jnp.concatenate([packed[:, 0:40], swapped[:, 0:40]], axis=1).reshape(HALF, 128)
        table = jnp.where(degree >= m, table, 0.0)
        rhs[p, :, 0:128] = table.astype(BF16)
        rhs[p, :, 128:256] = jnp.where(((degree + m) & 1) == 1, -table, table).astype(BF16)

    row_r = lax.broadcasted_iota(jnp.int32, (512, 128), 0) & 31
    j_r = row_r - GROUP * jnp.floor((row_r.astype(F32) + 0.5) * 0.2).astype(jnp.int32)
    slot_j[...] = j_r
    lane_r = lax.broadcasted_iota(jnp.int32, (32, 128), 1)
    pltpu.make_async_copy(recv_s, recv_s, ss_recv).wait()

    left = recv_s[...].reshape(512, HALF)
    terms = [jnp.dot(left, rhs[p], preferred_element_type=F32) for p in range(3)]
    j_r = slot_j[...]
    north, south = [
        jnp.where(j_r >= 4, terms[2][:, at:at + 128], jnp.where(j_r >= 2, terms[1][:, at:at + 128], terms[0][:, at:at + 128]))
        for at in (0, 128)
    ]
    odd = (j_r & 1) == 1
    north = jnp.where(odd, pltpu.roll(north, PAIRS, 1), north)
    south = jnp.where(odd, south, pltpu.roll(south, PAIRS, 1))
    both_halves = jnp.where(lane_r[0:1, :] < PAIRS, north, south)
    send_r[...] = both_halves.astype(BF16).reshape(LEVS, 32, 128)

    def level_copy(k):
        to = lax.rem(me + k, LEVS)
        return pltpu.make_async_remote_copy(
            src_ref=send_r.at[to], dst_ref=recv_x.at[me], send_sem=sx_send,
            recv_sem=sx_recv, device_id={"lev": to}, device_id_type=MESH,
        )

    for k in sorted(range(1, LEVS), key=lambda k: abs(k - LEVS // 2)):
        level_copy(k).start()
    pltpu.make_async_copy(send_r.at[me], recv_x.at[me], sx_recv).start()
    pltpu.make_async_copy(recv_x, recv_x, sx_recv).wait()

    got = recv_x[...].astype(F32).reshape(CHIPS, 2, 32, 128)
    level_sums = (got[:, 0] + got[:, 1]).reshape(256, 128).astype(BF16)
    by_slot = nt_dot(onehot[...], level_sums)
    low = by_slot[:, 0:128].reshape(WAVES, 8, 128)
    high = by_slot[:, 128:256].reshape(WAVES, 8, 128)
    send_y[...] = jnp.concatenate([low, high], axis=1).astype(BF16)

    def band_copy(k):
        to = lax.rem(w + k, WAVES)
        return pltpu.make_async_remote_copy(
            src_ref=send_y.at[to], dst_ref=recv_z.at[w], send_sem=sz_send,
            recv_sem=sz_recv, device_id={"wave": to}, device_id_type=MESH,
        )

    for k in sorted(range(1, WAVES), key=lambda k: abs(k - WAVES // 2)):
        band_copy(k).start()
    pltpu.make_async_copy(send_y.at[w], recv_z.at[w], sz_recv).start()
    pltpu.make_async_copy(recv_z, recv_z, sz_recv).wait()

    zf[...] = recv_z[...].astype(F32).reshape(512, 128)
    for slot in range(LAT_MAX):
        zs[64 * slot:64 * slot + 64, :] = zf[pl.ds(slot, 64, stride=8), :].astype(BF16)

    def modulate(i, carry):
        both = jnp.dot(zs[...], expand[i], preferred_element_type=F32)
        at = pl.multiple_of(64 * i, 64)
        other = pl.multiple_of(64 * i + MW, 64)
        for slot in range(LAT_MAX):
            re = both[64 * slot:64 * slot + 64, 0:128]
            im = both[64 * slot:64 * slot + 64, 128:256]
            cos_part = cosc[slot, pl.ds(at, 64), :]
            sin_part = sinc[slot, pl.ds(at, 64), :]
            mod[slot, pl.ds(at, 64), :] = (re * cos_part - im * sin_part).astype(BF16)
            mod[slot, pl.ds(other, 64), :] = (re * sin_part + im * cos_part).astype(BF16)
        return carry

    lax.fori_loop(0, 20, modulate, 0, unroll=20)

    def transform(slot, carry):
        points = jnp.dot(tw[slot], mod[slot], preferred_element_type=F32)
        lat[pl.ds(slot, 128, stride=8), :] = points.T
        return carry

    lax.fori_loop(0, LAT_MAX, transform, 0, unroll=8)

    slot_of = lax.broadcasted_iota(jnp.int32, (8, 128), 0)
    lon = lax.broadcasted_iota(jnp.int32, (8, 128), 1)
    cycles = jnp.zeros((8, 128), jnp.int32)
    for slot in range(LAT_MAX):
        cycles = jnp.where(slot_of == slot, cycle_of(slot), cycles)
    for f in range(3):
        for kh in range(KH):
            at = 8 * (KH * f + kh)
            width = min(128, NLON_MAX - 128 * kh)
            tile = jnp.where(lon + 128 * kh < cycles, lat[at:at + 8, :], 0.0).astype(BF16)
            out_ref[f, :, 128 * kh:128 * kh + width] = tile[:, 0:width]

    def all_sent(block, count, sem):
        part = block.at[pl.ds(0, count)]
        pltpu.make_async_copy(part, part, sem).wait()

    all_sent(recv_s, LEVS - 1, ss_send)

    @pl.when(c == half)
    def _():
        all_sent(recv_l, CHIPS - 1, sl_send)

    @pl.when(c != half)
    def _():
        all_sent(recv_l, CHIPS, sl_send)

    all_sent(recv_x, LEVS - 1, sx_send)
    all_sent(recv_z, WAVES - 1, sz_send)


def on_device(spec, legendre, mids, band_lats, nlon):
    spec_rows = spec.reshape(240, MW)
    tables = jnp.transpose(legendre, (0, 2, 1))
    hbm = pl.BlockSpec(memory_space=pltpu.HBM)
    vmem = pl.BlockSpec(memory_space=pltpu.VMEM)
    dma = pltpu.SemaphoreType.DMA
    planes = pl.pallas_call(
        kernel,
        out_shape=jax.ShapeDtypeStruct((3, LAT_MAX, NLON_MAX), BF16),
        in_specs=[hbm] * 6,
        out_specs=vmem,
        scratch_shapes=[
            pltpu.SMEM((MW,), jnp.int32),
            pltpu.SMEM((WAVES,), jnp.int32),
            pltpu.SMEM((PAIRS,), jnp.int32),
            pltpu.VMEM((240, MW), BF16),
            pltpu.VMEM((SLOTS, PAIRS, BLOCK), BF16),
            pltpu.VMEM((16, 128), jnp.int32),
            pltpu.VMEM((1, MW), F32),
            pltpu.VMEM((10, 256, 128), F32),
            pltpu.VMEM((CHIPS, 2, 32, HALF), BF16),
            pltpu.VMEM((CHIPS, LEG_ROWS, 128), BF16),
            pltpu.VMEM((LEVS, 32, HALF), BF16),
            pltpu.VMEM((8, LEG_ROWS, 128), BF16),
            pltpu.VMEM((3, HALF, 256), BF16),
            pltpu.VMEM((512, 128), jnp.int32),
            pltpu.VMEM((LEVS, 32, 128), BF16),
            pltpu.VMEM((LEVS, 32, 128), BF16),
            pltpu.VMEM((256, 128), BF16),
            pltpu.VMEM((WAVES, 16, 128), BF16),
            pltpu.VMEM((WAVES, 16, 128), BF16),
            pltpu.VMEM((512, 128), F32),
            pltpu.VMEM((512, 128), BF16),
            pltpu.VMEM((20, 128, 256), BF16),
            pltpu.VMEM((MW, 128), F32),
            pltpu.VMEM((LAT_MAX, MW, 128), F32),
            pltpu.VMEM((LAT_MAX, MW, 128), F32),
            pltpu.VMEM((LAT_MAX, 128, 2 * MW), BF16),
            pltpu.VMEM((LAT_MAX, 2 * MW, 128), BF16),
            pltpu.VMEM((1024, 128), F32),
            dma((6,)), dma, dma, dma, dma, dma, dma, dma, dma,
        ],
        compiler_params=pltpu.CompilerParams(
            collective_id=0, has_side_effects=True, vmem_limit_bytes=58 * 2**20
        ),
    )(mids, band_lats, nlon, spec_rows, tables, mids.reshape(10, 128))
    return jnp.transpose(planes, (1, 0, 2)).reshape(LAT_MAX, 3, 1, NLON_MAX)


def solution(mesh):
    in_specs = (P(None, None, "lev", "wave", None), P("wave", "lev", None), P(), P(), P())
    out_specs = P("wave", None, "lev", None)
    return jax.shard_map(
        on_device, mesh=mesh, in_specs=in_specs, out_specs=out_specs, check_vma=False
    )
```

```python
import jax
import jax.numpy as jnp
from jax import lax
from jax.experimental import pallas as pl
from jax.experimental.pallas import tpu as pltpu
from jax.sharding import PartitionSpec as P

LAT_MAX = 8
NLON_MAX = 5136
KH = 41
WAVES = 32
LEVS = 16
CHIPS = 8
SLOTS = 40
GROUP = 5
MW = 1280
BLOCK = 80
LEG_ROWS = 208
PAIRS = 64
LATS = 128
TWO_PI = 6.283185307179586
F32 = jnp.float32
BF16 = jnp.bfloat16
MESH = pl.DeviceIdType.MESH

SIN = []
_term = TWO_PI
for _i in range(6):
    SIN.append(_term)
    _term = -_term * TWO_PI * TWO_PI / ((2 * _i + 2) * (2 * _i + 3))


def quarter_sine(y):
    y2 = y * y
    acc = jnp.full_like(y2, SIN[-1])
    for c in SIN[-2::-1]:
        acc = acc * y2 + c
    return acc * y


def cos_sin(steps, cycle, inverse):
    rest = steps - jnp.floor(steps * inverse + 0.5) * cycle
    t = rest * inverse
    a = jnp.abs(t)
    folded = jnp.where(a > 0.25, jnp.where(t < 0, -0.5, 0.5) - t, t)
    return quarter_sine(0.25 - a), quarter_sine(folded)


def nt_dot(a, b):
    return lax.dot_general(a, b, (((1,), (1,)), ((), ())), preferred_element_type=F32)


def kernel(
    mids_hbm, bands_hbm, nlon_hbm, spec_hbm, leg_hbm, mids_rows_hbm, out_ref,
    mids_ref, bands_ref, nlon_ref, spec_ref, leg_ref, mids_rows, mrow_ref, spec_f, send_s, send_l, recv_s, recv_l, rhs, slot_j, send_r, recv_x,
    onehot, send_y, recv_z, zf, zs, expand, mcol, cosc, sinc, tw, mod, lat,
    load_sem, ss_send, ss_recv, sl_send, sl_recv, sf_send, sf_recv, sx_send, sx_recv, sz_send, sz_recv,
):
    w = lax.axis_index("wave")
    me = lax.axis_index("lev")
    z = me // 2
    c = me - 2 * z

    mids_rows[...] = jnp.zeros_like(mids_rows)
    loads = [
        pltpu.make_async_copy(leg_hbm, leg_ref, load_sem.at[0]),
        pltpu.make_async_copy(spec_hbm, spec_ref, load_sem.at[1]),
        pltpu.make_async_copy(mids_rows_hbm, mids_rows.at[0:10], load_sem.at[2]),
        pltpu.make_async_copy(mids_hbm, mids_ref, load_sem.at[3]),
        pltpu.make_async_copy(bands_hbm, bands_ref, load_sem.at[4]),
        pltpu.make_async_copy(nlon_hbm, nlon_ref, load_sem.at[5]),
    ]
    for load in loads:
        load.start()

    barrier = pltpu.get_barrier_semaphore()
    for k in sorted(range(1, CHIPS), key=lambda k: abs(k - CHIPS // 2)):
        peer = 2 * lax.rem(z + k, CHIPS) + c
        pl.semaphore_signal(barrier, inc=1, device_id={"lev": peer}, device_id_type=MESH)
    sibling = 2 * z + (1 - c)
    pl.semaphore_signal(barrier, inc=1, device_id={"lev": sibling}, device_id_type=MESH)
    for k in range(1, WAVES):
        pl.semaphore_signal(barrier, inc=1, device_id={"wave": lax.rem(w + k, WAVES)}, device_id_type=MESH)


    unit = jnp.where(
        lax.broadcasted_iota(jnp.int32, (BLOCK, BLOCK), 0) == lax.broadcasted_iota(jnp.int32, (BLOCK, BLOCK), 1),
        1.0, 0.0,
    ).astype(BF16)

    fold = jnp.where(
        (lax.broadcasted_iota(jnp.int32, (48, BLOCK), 0) == lax.broadcasted_iota(jnp.int32, (48, BLOCK), 1))
        | (lax.broadcasted_iota(jnp.int32, (48, BLOCK), 0) + 40 == lax.broadcasted_iota(jnp.int32, (48, BLOCK), 1)),
        1.0, 0.0,
    )
    fold = jnp.where(lax.broadcasted_iota(jnp.int32, (48, BLOCK), 0) < 40, fold, 0.0).astype(BF16)
    upper = (lax.broadcasted_iota(jnp.int32, (LATS, BLOCK), 0) < PAIRS) == (
        lax.broadcasted_iota(jnp.int32, (LATS, BLOCK), 1) < 40
    )
    loads[0].wait()
    pl.semaphore_wait(barrier, CHIPS + WAVES - 1)

    def spec_copy(k):
        to = lax.rem(z + k, CHIPS)
        return pltpu.make_async_remote_copy(
            src_ref=send_s.at[to], dst_ref=recv_s.at[z], send_sem=ss_send,
            recv_sem=ss_recv, device_id={"lev": 2 * to + c}, device_id_type=MESH,
        )

    def leg_copy(k):
        to = lax.rem(z + k, CHIPS)
        return pltpu.make_async_remote_copy(
            src_ref=send_l.at[to], dst_ref=recv_l.at[c, z], send_sem=sl_send,
            recv_sem=sl_recv.at[z], device_id={"lev": 2 * to + c}, device_id_type=MESH,
        )

    def share_copy(chip):
        return pltpu.make_async_remote_copy(
            src_ref=recv_l.at[c, chip], dst_ref=recv_l.at[c, chip], send_sem=sf_send,
            recv_sem=sf_recv, device_id={"lev": sibling}, device_id_type=MESH,
        )

    def order_of(i):
        return jnp.where(lax.rem(i, 2) == 1, 4 - (i + 1) // 2, 4 + i // 2)

    def prepare_leg(k):
        to = lax.rem(z + k, CHIPS)
        for p in range(2):
            stacked = jnp.concatenate([leg_ref[16 * p + to], leg_ref[16 * p + 8 + to]], axis=0)
            send_l[to, BLOCK * p:BLOCK * p + BLOCK, :] = nt_dot(unit, stacked).astype(BF16)
        last = leg_ref[32 + to].astype(F32)
        stacked = jnp.where(upper, jnp.concatenate([last, last], axis=0), 0.0).astype(BF16)
        send_l[to, 2 * BLOCK:LEG_ROWS, :] = nt_dot(fold, stacked).astype(BF16)

    def prepare_spec(k):
        to = lax.rem(z + k, CHIPS)
        for tile in range(10):
            rows = spec_f[tile, pl.ds(to, 32, stride=8), :].astype(BF16)
            send_s[to, :, 128 * tile:128 * tile + 128] = rows

    def send_leg(i, carry):
        k = order_of(i)
        prepare_leg(k)
        leg_copy(k).start()
        return carry

    lax.fori_loop(0, CHIPS - 1, send_leg, 0)
    prepare_leg(0)

    pltpu.make_async_copy(send_l.at[z], recv_l.at[c, z], sl_recv.at[z]).start()

    loads[1].wait()
    for tile in range(10):
        spec_f[tile, 0:240, :] = spec_ref[:, 128 * tile:128 * tile + 128].astype(F32)
        spec_f[tile, 240:256, :] = jnp.zeros((16, 128), F32)

    def send_spec(i, carry):
        k = order_of(i)
        prepare_spec(k)
        spec_copy(k).start()
        return carry

    lax.fori_loop(0, CHIPS - 1, send_spec, 0)
    prepare_spec(0)
    pltpu.make_async_copy(send_s.at[z], recv_s.at[z], ss_recv).start()

    for load in loads[2:]:
        load.wait()

    start = jnp.int32(0)
    own_start = jnp.int32(0)
    sub16 = lax.broadcasted_iota(jnp.int32, (16, 128), 0)
    lane = lax.broadcasted_iota(jnp.int32, (16, 128), 1)
    lat_of = jnp.where(lane < PAIRS, lane, LATS - 1 - (lane - PAIRS))
    for e in range(WAVES // 2):
        count_a, count_b = bands_ref[2 * e], bands_ref[2 * e + 1]
        start_b = start + count_a
        own_start = jnp.where(w == 2 * e, start, jnp.where(w == 2 * e + 1, start_b, own_start))
        inner = sub16 & 7
        wanted = jnp.where(sub16 < 8, start, start_b) + inner
        filled = inner < jnp.where(sub16 < 8, count_a, count_b)
        match = jnp.where(filled, wanted, -1) == lat_of
        onehot[16 * e:16 * e + 16, :] = jnp.where(match, 1.0, 0.0).astype(BF16)
        start = start_b + count_b

    def cycle_of(slot):
        latitude = jnp.minimum(own_start + slot, LATS - 1)
        pair = jnp.where(latitude < PAIRS, latitude, LATS - 1 - latitude)
        return nlon_ref[pair]

    krow = lax.broadcasted_iota(jnp.int32, (128, 256), 0)
    klane = lax.broadcasted_iota(jnp.int32, (128, 256), 1)
    col = klane & 127
    channel = jnp.where(col >= KH, 1, 0) + jnp.where(col >= 2 * KH, 1, 0) + jnp.where(col >= 3 * KH, 100, 0)
    base = krow - (GROUP * channel + jnp.where(klane >= 128, 15, 0))

    def fill_expand(i, carry):
        zl = i // GROUP
        match = base == zl * 32 + (i - GROUP * zl)
        expand[i] = jnp.where(match, 1.0, 0.0).astype(BF16)
        return carry

    lax.fori_loop(0, 20, fill_expand, 0)

    natural = mids_rows[...].astype(F32)
    high = jnp.floor(natural * 0.125)
    digits = jnp.concatenate([high, natural - 8.0 * high], axis=0).astype(BF16)
    for t in range(10):
        place = lax.broadcasted_iota(jnp.int32, (128, 128), 1) + 128 * t
        group = place >> 6
        zl = jnp.where(group >= 5, 1, 0) + jnp.where(group >= 10, 1, 0) + jnp.where(group >= 15, 1, 0)
        source = SLOTS * ((place & 63) >> 1) + 8 * (group - GROUP * zl) + 4 * (place & 1) + zl
        pick = lax.broadcasted_iota(jnp.int32, (128, 128), 0) == (source & 127)
        found = jnp.dot(digits, jnp.where(pick, 1.0, 0.0).astype(BF16), preferred_element_type=F32)
        found = 8.0 * found[0:16, :] + found[16:32, :]
        here = lax.broadcasted_iota(jnp.int32, (16, 128), 0) == (source[0:16, :] >> 7)
        row = jnp.sum(jnp.where(here, found, 0.0), axis=0, keepdims=True)
        mrow_ref[0:1, 128 * t:128 * t + 128] = row
        mcol[128 * t:128 * t + 128, :] = jnp.broadcast_to(row, (128, 128)).T

    col1 = lax.broadcasted_iota(jnp.int32, (1, 128), 1)
    channel1 = jnp.where(col1 >= KH, 1, 0) + jnp.where(col1 >= 2 * KH, 1, 0)
    coarse_steps = (128 * (col1 - KH * channel1)).astype(F32)
    a_steps = (16 * lax.broadcasted_iota(jnp.int32, (8, 128), 0)).astype(F32)
    b_steps = lax.broadcasted_iota(jnp.int32, (16, 128), 0).astype(F32)

    def tables(slot, carry):
        cycle = jnp.full((1, 128), cycle_of(slot), jnp.int32).astype(F32)
        inverse = 1.0 / cycle

        def coarse(i, inner_carry):
            at = pl.multiple_of(128 * i, 128)
            cos_part, sin_part = cos_sin(mcol[pl.ds(at, 128), :] * coarse_steps, cycle, inverse)
            cosc[slot, pl.ds(at, 128), :] = cos_part
            sinc[slot, pl.ds(at, 128), :] = sin_part
            return inner_carry

        lax.fori_loop(0, 10, coarse, 0)

        def fine(i, inner_carry):
            at = pl.multiple_of(128 * i, 128)
            m = mrow_ref[0:1, pl.ds(at, 128)]
            weight = jnp.where(m == 0, 1.0, 2.0)
            weight = jnp.where(2 * m < cycle, weight, 0.0)
            cos_a, sin_a = cos_sin(m * a_steps, cycle, inverse)
            cos_b, sin_b = cos_sin(m * b_steps, cycle, inverse)
            cos_a = cos_a * weight
            sin_a = sin_a * weight
            for a in range(8):
                ca, sa = cos_a[a:a + 1, :], sin_a[a:a + 1, :]
                tw[slot, 16 * a:16 * a + 16, pl.ds(at, 128)] = (ca * cos_b - sa * sin_b).astype(BF16)
                other = pl.multiple_of(at + MW, 128)
                tw[slot, 16 * a:16 * a + 16, pl.ds(other, 128)] = (-(sa * cos_b + ca * sin_b)).astype(BF16)
            return inner_carry

        lax.fori_loop(0, 10, fine, 0)
        return carry

    lax.fori_loop(0, LAT_MAX, tables, 0)

    def share(i, carry):
        chip = lax.rem(z - jnp.where(i == CHIPS - 1, 0, order_of(i)) + CHIPS, CHIPS)
        pltpu.make_async_copy(recv_l.at[c, chip], recv_l.at[c, chip], sl_recv.at[chip]).wait()
        share_copy(chip).start()
        return carry

    lax.fori_loop(0, CHIPS, share, 0)
    pltpu.make_async_copy(recv_l.at[1 - c], recv_l.at[1 - c], sf_recv).wait()
    degree = lax.broadcasted_iota(jnp.int32, (MW, 128), 0)
    lane_n = lax.broadcasted_iota(jnp.int32, (MW, 128), 1)
    for p in range(3):
        m_a = mids_ref[SLOTS * w + 16 * p + z]
        m_b = mids_ref[SLOTS * w + 16 * p + 8 + z] if p < 2 else m_a
        m = jnp.where(lane_n < PAIRS, m_a, m_b)
        parts = []
        for core in range(2):
            if p < 2:
                parts.append(recv_l[core, :, BLOCK * p:BLOCK * p + BLOCK, :].astype(F32))
            else:
                packed = recv_l[core, :, 2 * BLOCK:LEG_ROWS, :].astype(F32)
                swapped = jnp.concatenate([packed[:, :, 64:128], packed[:, :, 0:64]], axis=2)
                parts += [packed[:, 0:40], swapped[:, 0:40]]
        table = jnp.concatenate(parts, axis=1).reshape(MW, 128)
        table = jnp.where(degree >= m, table, 0.0)
        rhs[p, :, 0:128] = table.astype(BF16)
        rhs[p, :, 128:256] = jnp.where(((degree + m) & 1) == 1, -table, table).astype(BF16)

    row_r = lax.broadcasted_iota(jnp.int32, (256, 128), 0) & 31
    j_r = row_r - GROUP * jnp.floor((row_r.astype(F32) + 0.5) * 0.2).astype(jnp.int32)
    slot_j[...] = j_r
    lane_r = lax.broadcasted_iota(jnp.int32, (32, 128), 1)
    pltpu.make_async_copy(recv_s, recv_s, ss_recv).wait()

    left = recv_s[...].reshape(256, MW)
    terms = [jnp.dot(left, rhs[p], preferred_element_type=F32) for p in range(3)]
    j_r = slot_j[...]
    north, south = [
        jnp.where(j_r >= 4, terms[2][:, at:at + 128], jnp.where(j_r >= 2, terms[1][:, at:at + 128], terms[0][:, at:at + 128]))
        for at in (0, 128)
    ]
    odd = (j_r & 1) == 1
    north = jnp.where(odd, pltpu.roll(north, PAIRS, 1), north)
    south = jnp.where(odd, south, pltpu.roll(south, PAIRS, 1))
    both_halves = jnp.where(lane_r[0:1, :] < PAIRS, north, south)
    send_r[...] = both_halves.astype(BF16).reshape(CHIPS, 32, 128)

    def level_copy(k):
        to = lax.rem(z + k, CHIPS)
        return pltpu.make_async_remote_copy(
            src_ref=send_r.at[to], dst_ref=recv_x.at[z], send_sem=sx_send,
            recv_sem=sx_recv, device_id={"lev": 2 * to + c}, device_id_type=MESH,
        )

    for k in sorted(range(1, CHIPS), key=lambda k: abs(k - CHIPS // 2)):
        level_copy(k).start()
    pltpu.make_async_copy(send_r.at[z], recv_x.at[z], sx_recv).start()
    pltpu.make_async_copy(recv_x, recv_x, sx_recv).wait()

    level_sums = recv_x[...].reshape(256, 128)
    by_slot = nt_dot(onehot[...], level_sums)
    low = by_slot[:, 0:128].reshape(WAVES, 8, 128)
    high = by_slot[:, 128:256].reshape(WAVES, 8, 128)
    send_y[...] = jnp.concatenate([low, high], axis=1).astype(BF16)

    def band_copy(k):
        to = lax.rem(w + k, WAVES)
        return pltpu.make_async_remote_copy(
            src_ref=send_y.at[to], dst_ref=recv_z.at[w], send_sem=sz_send,
            recv_sem=sz_recv, device_id={"wave": to}, device_id_type=MESH,
        )

    for k in sorted(range(1, WAVES), key=lambda k: abs(k - WAVES // 2)):
        band_copy(k).start()
    pltpu.make_async_copy(send_y.at[w], recv_z.at[w], sz_recv).start()
    pltpu.make_async_copy(recv_z, recv_z, sz_recv).wait()

    zf[...] = recv_z[...].astype(F32).reshape(512, 128)
    for slot in range(LAT_MAX):
        zs[64 * slot:64 * slot + 64, :] = zf[pl.ds(slot, 64, stride=8), :].astype(BF16)

    def modulate(i, carry):
        both = jnp.dot(zs[...], expand[i], preferred_element_type=F32)
        at = pl.multiple_of(64 * i, 64)
        other = pl.multiple_of(64 * i + MW, 64)
        for slot in range(LAT_MAX):
            re = both[64 * slot:64 * slot + 64, 0:128]
            im = both[64 * slot:64 * slot + 64, 128:256]
            cos_part = cosc[slot, pl.ds(at, 64), :]
            sin_part = sinc[slot, pl.ds(at, 64), :]
            mod[slot, pl.ds(at, 64), :] = (re * cos_part - im * sin_part).astype(BF16)
            mod[slot, pl.ds(other, 64), :] = (re * sin_part + im * cos_part).astype(BF16)
        return carry

    lax.fori_loop(0, 20, modulate, 0, unroll=20)

    def transform(slot, carry):
        points = jnp.dot(tw[slot], mod[slot], preferred_element_type=F32)
        lat[pl.ds(slot, 128, stride=8), :] = points.T
        return carry

    lax.fori_loop(0, LAT_MAX, transform, 0, unroll=8)

    slot_of = lax.broadcasted_iota(jnp.int32, (8, 128), 0)
    lon = lax.broadcasted_iota(jnp.int32, (8, 128), 1)
    cycles = jnp.zeros((8, 128), jnp.int32)
    for slot in range(LAT_MAX):
        cycles = jnp.where(slot_of == slot, cycle_of(slot), cycles)
    for f in range(3):
        for kh in range(KH):
            at = 8 * (KH * f + kh)
            width = min(128, NLON_MAX - 128 * kh)
            tile = jnp.where(lon + 128 * kh < cycles, lat[at:at + 8, :], 0.0).astype(BF16)
            out_ref[f, :, 128 * kh:128 * kh + width] = tile[:, 0:width]

    def all_sent(block, count, sem):
        part = block.at[pl.ds(0, count)]
        pltpu.make_async_copy(part, part, sem).wait()

    all_sent(recv_s, CHIPS - 1, ss_send)
    all_sent(recv_l.at[0], CHIPS - 1, sl_send)
    all_sent(recv_l.at[0], CHIPS, sf_send)
    all_sent(recv_x, CHIPS - 1, sx_send)
    all_sent(recv_z, WAVES - 1, sz_send)


def on_device(spec, legendre, mids, band_lats, nlon):
    spec_rows = spec.reshape(240, MW)
    tables = jnp.transpose(legendre, (0, 2, 1))
    hbm = pl.BlockSpec(memory_space=pltpu.HBM)
    vmem = pl.BlockSpec(memory_space=pltpu.VMEM)
    dma = pltpu.SemaphoreType.DMA
    planes = pl.pallas_call(
        kernel,
        out_shape=jax.ShapeDtypeStruct((3, LAT_MAX, NLON_MAX), BF16),
        in_specs=[hbm] * 6,
        out_specs=vmem,
        scratch_shapes=[
            pltpu.SMEM((MW,), jnp.int32),
            pltpu.SMEM((WAVES,), jnp.int32),
            pltpu.SMEM((PAIRS,), jnp.int32),
            pltpu.VMEM((240, MW), BF16),
            pltpu.VMEM((SLOTS, PAIRS, BLOCK), BF16),
            pltpu.VMEM((16, 128), jnp.int32),
            pltpu.VMEM((1, MW), F32),
            pltpu.VMEM((10, 256, 128), F32),
            pltpu.VMEM((CHIPS, 32, MW), BF16),
            pltpu.VMEM((CHIPS, LEG_ROWS, 128), BF16),
            pltpu.VMEM((CHIPS, 32, MW), BF16),
            pltpu.VMEM((2, CHIPS, LEG_ROWS, 128), BF16),
            pltpu.VMEM((3, MW, 256), BF16),
            pltpu.VMEM((256, 128), jnp.int32),
            pltpu.VMEM((CHIPS, 32, 128), BF16),
            pltpu.VMEM((CHIPS, 32, 128), BF16),
            pltpu.VMEM((256, 128), BF16),
            pltpu.VMEM((WAVES, 16, 128), BF16),
            pltpu.VMEM((WAVES, 16, 128), BF16),
            pltpu.VMEM((512, 128), F32),
            pltpu.VMEM((512, 128), BF16),
            pltpu.VMEM((20, 128, 256), BF16),
            pltpu.VMEM((MW, 128), F32),
            pltpu.VMEM((LAT_MAX, MW, 128), F32),
            pltpu.VMEM((LAT_MAX, MW, 128), F32),
            pltpu.VMEM((LAT_MAX, 128, 2 * MW), BF16),
            pltpu.VMEM((LAT_MAX, 2 * MW, 128), BF16),
            pltpu.VMEM((1024, 128), F32),
            dma((6,)), dma, dma, dma, dma((CHIPS,)), dma, dma, dma, dma, dma, dma,
        ],
        compiler_params=pltpu.CompilerParams(
            collective_id=0, has_side_effects=True, vmem_limit_bytes=58 * 2**20
        ),
    )(mids, band_lats, nlon, spec_rows, tables, mids.reshape(10, 128))
    return jnp.transpose(planes, (1, 0, 2)).reshape(LAT_MAX, 3, 1, NLON_MAX)


def solution(mesh):
    in_specs = (P(None, None, "lev", "wave", None), P("wave", "lev", None), P(), P(), P())
    out_specs = P("wave", None, "lev", None)
    return jax.shard_map(
        on_device, mesh=mesh, in_specs=in_specs, out_specs=out_specs, check_vma=False
    )
```

```python
import jax
import jax.numpy as jnp
from jax import lax
from jax.experimental import pallas as pl
from jax.experimental.pallas import tpu as pltpu
from jax.sharding import PartitionSpec as P

LAT_MAX = 8
NLON_MAX = 5136
KH = 41
WAVES = 32
LEVS = 16
CHIPS = 8
SLOTS = 40
GROUP = 5
HALF = 640
MW = 1280
BLOCK = 80
LEG_ROWS = 208
PAIRS = 64
LATS = 128
TWO_PI = 6.283185307179586
F32 = jnp.float32
BF16 = jnp.bfloat16
MESH = pl.DeviceIdType.MESH

SIN = []
_term = TWO_PI
for _i in range(6):
    SIN.append(_term)
    _term = -_term * TWO_PI * TWO_PI / ((2 * _i + 2) * (2 * _i + 3))


def quarter_sine(y):
    y2 = y * y
    acc = jnp.full_like(y2, SIN[-1])
    for c in SIN[-2::-1]:
        acc = acc * y2 + c
    return acc * y


def cos_sin(steps, cycle, inverse):
    rest = steps - jnp.floor(steps * inverse + 0.5) * cycle
    t = rest * inverse
    a = jnp.abs(t)
    folded = jnp.where(a > 0.25, jnp.where(t < 0, -0.5, 0.5) - t, t)
    return quarter_sine(0.25 - a), quarter_sine(folded)


def nt_dot(a, b):
    return lax.dot_general(a, b, (((1,), (1,)), ((), ())), preferred_element_type=F32)


def kernel(
    mids_hbm, bands_hbm, nlon_hbm, spec_hbm, leg_hbm, mids_rows_hbm, out_ref,
    mids_ref, bands_ref, nlon_ref, spec_ref, leg_ref, mids_rows, mrow_ref, spec_f, send_s, send_l, recv_s, recv_l, rhs, slot_j, send_r, recv_x,
    onehot, send_y, recv_z, zf, zs, expand, mcol, cosc, sinc, tw, mod, partial, lat,
    load_sem, ss_send, ss_recv, sl_send, sl_recv, sf_send, sf_recv, sx_send, sx_recv, sz_send, sz_recv,
):
    w = lax.axis_index("wave")
    me = lax.axis_index("lev")
    z = me // 2
    c = me - 2 * z

    mids_rows[...] = jnp.zeros_like(mids_rows)
    loads = [
        pltpu.make_async_copy(leg_hbm, leg_ref, load_sem.at[0]),
        pltpu.make_async_copy(spec_hbm, spec_ref, load_sem.at[1]),
        pltpu.make_async_copy(mids_rows_hbm, mids_rows.at[0:10], load_sem.at[2]),
        pltpu.make_async_copy(mids_hbm, mids_ref, load_sem.at[3]),
        pltpu.make_async_copy(bands_hbm, bands_ref, load_sem.at[4]),
        pltpu.make_async_copy(nlon_hbm, nlon_ref, load_sem.at[5]),
    ]
    for load in loads:
        load.start()

    barrier = pltpu.get_barrier_semaphore()
    for k in sorted(range(1, CHIPS), key=lambda k: abs(k - CHIPS // 2)):
        peer = 2 * lax.rem(z + k, CHIPS) + c
        pl.semaphore_signal(barrier, inc=1, device_id={"lev": peer}, device_id_type=MESH)
    sibling = 2 * z + (1 - c)
    pl.semaphore_signal(barrier, inc=1, device_id={"lev": sibling}, device_id_type=MESH)
    for k in range(1, WAVES):
        pl.semaphore_signal(barrier, inc=1, device_id={"wave": lax.rem(w + k, WAVES)}, device_id_type=MESH)


    unit = jnp.where(
        lax.broadcasted_iota(jnp.int32, (BLOCK, BLOCK), 0) == lax.broadcasted_iota(jnp.int32, (BLOCK, BLOCK), 1),
        1.0, 0.0,
    ).astype(BF16)

    fold = jnp.where(
        (lax.broadcasted_iota(jnp.int32, (48, BLOCK), 0) == lax.broadcasted_iota(jnp.int32, (48, BLOCK), 1))
        | (lax.broadcasted_iota(jnp.int32, (48, BLOCK), 0) + 40 == lax.broadcasted_iota(jnp.int32, (48, BLOCK), 1)),
        1.0, 0.0,
    )
    fold = jnp.where(lax.broadcasted_iota(jnp.int32, (48, BLOCK), 0) < 40, fold, 0.0).astype(BF16)
    upper = (lax.broadcasted_iota(jnp.int32, (LATS, BLOCK), 0) < PAIRS) == (
        lax.broadcasted_iota(jnp.int32, (LATS, BLOCK), 1) < 40
    )
    loads[0].wait()
    pl.semaphore_wait(barrier, CHIPS + WAVES - 1)

    def first_chip(chip):
        return (chip + 6 + (chip & 1)) & 7

    own_first = first_chip(z)

    def spec_copy(k):
        to = lax.rem(z + k, CHIPS)
        return pltpu.make_async_remote_copy(
            src_ref=send_s.at[to], dst_ref=recv_s.at[z], send_sem=ss_send,
            recv_sem=ss_recv, device_id={"lev": 2 * to + c}, device_id_type=MESH,
        )

    def leg_copy(to):
        seat = (z - first_chip(to)) & 7
        return pltpu.make_async_remote_copy(
            src_ref=send_l.at[to & 3], dst_ref=recv_l.at[c, seat], send_sem=sl_send,
            recv_sem=sl_recv.at[seat], device_id={"lev": 2 * to + c}, device_id_type=MESH,
        )

    def share_copy(seat):
        return pltpu.make_async_remote_copy(
            src_ref=recv_l.at[c, seat], dst_ref=recv_l.at[c, seat], send_sem=sf_send,
            recv_sem=sf_recv, device_id={"lev": sibling}, device_id_type=MESH,
        )

    def order_of(i):
        return jnp.where(lax.rem(i, 2) == 1, 4 - (i + 1) // 2, 4 + i // 2)

    def prepare_leg(low, gi):
        group = low + 4 * gi
        for p in range(2):
            stacked = jnp.concatenate([leg_ref[16 * p + group], leg_ref[16 * p + 8 + group]], axis=0)
            send_l[low, gi, BLOCK * p:BLOCK * p + BLOCK, :] = nt_dot(unit, stacked).astype(BF16)
        last = leg_ref[32 + group].astype(F32)
        stacked = jnp.where(upper, jnp.concatenate([last, last], axis=0), 0.0).astype(BF16)
        send_l[low, gi, 2 * BLOCK:LEG_ROWS, :] = nt_dot(fold, stacked).astype(BF16)

    lane_s = lax.broadcasted_iota(jnp.int32, (32, 128), 1)

    def prepare_spec(k):
        to = lax.rem(z + k, CHIPS)
        start = 2 * BLOCK * first_chip(to)
        shift = start & 127
        for gi in range(2):
            turned = []
            for u in range(6):
                tile = lax.rem((start >> 7) + u, 10)
                rows = spec_f[tile, pl.ds((to & 3) + 4 * gi, 32, stride=8), :]
                turned.append(pltpu.roll(rows, (128 - shift) & 127, 1))
            for u in range(5):
                rows = jnp.where(lane_s < 128 - shift, turned[u], turned[u + 1])
                send_s[to, 32 * gi:32 * gi + 32, 128 * u:128 * u + 128] = rows.astype(BF16)

    for to in ((z + 2 - 4 * (z & 1)) & 7, (z + 1) & 7, (z + 7) & 7):
        for gi in range(2):
            prepare_leg(to & 3, gi)
        leg_copy(to).start()
    for gi in range(2):
        prepare_leg(z & 3, gi)
    own_seat = (z - own_first) & 7
    pltpu.make_async_copy(send_l.at[z & 3], recv_l.at[c, own_seat], sl_recv.at[own_seat]).start()

    loads[1].wait()
    for tile in range(10):
        spec_f[tile, 0:240, :] = spec_ref[:, 128 * tile:128 * tile + 128].astype(F32)
        spec_f[tile, 240:256, :] = jnp.zeros((16, 128), F32)

    def send_spec(i, carry):
        k = order_of(i)
        prepare_spec(k)
        spec_copy(k).start()
        return carry

    lax.fori_loop(0, CHIPS - 1, send_spec, 0)
    prepare_spec(0)
    pltpu.make_async_copy(send_s.at[z], recv_s.at[z], ss_recv).start()

    for load in loads[2:]:
        load.wait()

    start = jnp.int32(0)
    own_start = jnp.int32(0)
    sub16 = lax.broadcasted_iota(jnp.int32, (16, 128), 0)
    lane = lax.broadcasted_iota(jnp.int32, (16, 128), 1)
    lat_of = jnp.where(lane < PAIRS, lane, LATS - 1 - (lane - PAIRS))
    for e in range(WAVES // 2):
        count_a, count_b = bands_ref[2 * e], bands_ref[2 * e + 1]
        start_b = start + count_a
        own_start = jnp.where(w == 2 * e, start, jnp.where(w == 2 * e + 1, start_b, own_start))
        inner = sub16 & 7
        wanted = jnp.where(sub16 < 8, start, start_b) + inner
        filled = inner < jnp.where(sub16 < 8, count_a, count_b)
        match = jnp.where(filled, wanted, -1) == lat_of
        onehot[16 * e:16 * e + 16, :] = jnp.where(match, 1.0, 0.0).astype(BF16)
        start = start_b + count_b

    def cycle_of(slot):
        latitude = jnp.minimum(own_start + slot, LATS - 1)
        pair = jnp.where(latitude < PAIRS, latitude, LATS - 1 - latitude)
        return nlon_ref[pair]

    krow = lax.broadcasted_iota(jnp.int32, (128, 256), 0)
    klane = lax.broadcasted_iota(jnp.int32, (128, 256), 1)
    col = klane & 127
    channel = jnp.where(col >= KH, 1, 0) + jnp.where(col >= 2 * KH, 1, 0) + jnp.where(col >= 3 * KH, 100, 0)
    base = krow - (GROUP * channel + jnp.where(klane >= 128, 15, 0))

    def fill_expand(i, carry):
        zl = i // GROUP
        match = base == zl * 32 + (i - GROUP * zl)
        expand[i] = jnp.where(match, 1.0, 0.0).astype(BF16)
        return carry

    lax.fori_loop(0, 20, fill_expand, 0)

    natural = mids_rows[...].astype(F32)
    high = jnp.floor(natural * 0.125)
    digits = jnp.concatenate([high, natural - 8.0 * high], axis=0).astype(BF16)
    for t in range(10):
        place = lax.broadcasted_iota(jnp.int32, (128, 128), 1) + 128 * t
        wave_half = jnp.where(place >= HALF, 1, 0)
        inner = place - HALF * wave_half
        group = inner >> 5
        zl = jnp.where(group >= 5, 1, 0) + jnp.where(group >= 10, 1, 0) + jnp.where(group >= 15, 1, 0)
        seat = (inner & 31) >> 1
        from_y = (w // 4 - (2 * (seat >> 2) + wave_half) + 8) & 7
        from_x = ((w & 3) - (seat & 3) + 4) & 3
        source = SLOTS * (4 * from_y + from_x) + 8 * (group - GROUP * zl) + 4 * (place & 1) + zl
        pick = lax.broadcasted_iota(jnp.int32, (128, 128), 0) == (source & 127)
        found = jnp.dot(digits, jnp.where(pick, 1.0, 0.0).astype(BF16), preferred_element_type=F32)
        found = 8.0 * found[0:16, :] + found[16:32, :]
        here = lax.broadcasted_iota(jnp.int32, (16, 128), 0) == (source[0:16, :] >> 7)
        row = jnp.sum(jnp.where(here, found, 0.0), axis=0, keepdims=True)
        mrow_ref[0:1, 128 * t:128 * t + 128] = row
        mcol[128 * t:128 * t + 128, :] = jnp.broadcast_to(row, (128, 128)).T

    col1 = lax.broadcasted_iota(jnp.int32, (1, 128), 1)
    channel1 = jnp.where(col1 >= KH, 1, 0) + jnp.where(col1 >= 2 * KH, 1, 0)
    coarse_steps = (128 * (col1 - KH * channel1)).astype(F32)
    a_steps = (16 * lax.broadcasted_iota(jnp.int32, (8, 128), 0)).astype(F32)
    b_steps = lax.broadcasted_iota(jnp.int32, (16, 128), 0).astype(F32)

    def tables(slot, carry):
        cycle = jnp.full((1, 128), cycle_of(slot), jnp.int32).astype(F32)
        inverse = 1.0 / cycle

        def coarse(i, inner_carry):
            at = pl.multiple_of(128 * i, 128)
            cos_part, sin_part = cos_sin(mcol[pl.ds(at, 128), :] * coarse_steps, cycle, inverse)
            cosc[slot, pl.ds(at, 128), :] = cos_part
            sinc[slot, pl.ds(at, 128), :] = sin_part
            return inner_carry

        lax.fori_loop(0, 10, coarse, 0)

        def fine(i, inner_carry):
            m = mrow_ref[0:1, pl.ds(pl.multiple_of(128 * i, 128), 128)]
            at = pl.multiple_of(128 * i + jnp.where(i >= 5, HALF, 0), 128)
            weight = jnp.where(m == 0, 1.0, 2.0)
            weight = jnp.where(2 * m < cycle, weight, 0.0)
            cos_a, sin_a = cos_sin(m * a_steps, cycle, inverse)
            cos_b, sin_b = cos_sin(m * b_steps, cycle, inverse)
            cos_a = cos_a * weight
            sin_a = sin_a * weight
            for a in range(8):
                ca, sa = cos_a[a:a + 1, :], sin_a[a:a + 1, :]
                tw[slot, 16 * a:16 * a + 16, pl.ds(at, 128)] = (ca * cos_b - sa * sin_b).astype(BF16)
                other = pl.multiple_of(at + HALF, 128)
                tw[slot, 16 * a:16 * a + 16, pl.ds(other, 128)] = (-(sa * cos_b + ca * sin_b)).astype(BF16)
            return inner_carry

        lax.fori_loop(0, 10, fine, 0)
        return carry

    lax.fori_loop(0, LAT_MAX, tables, 0)

    for seat in range(4):
        pltpu.make_async_copy(recv_l.at[c, seat], recv_l.at[c, seat], sl_recv.at[seat]).wait()
        share_copy(seat).start()
    pltpu.make_async_copy(recv_l.at[1 - c], recv_l.at[1 - c], sf_recv).wait()
    degree = lax.broadcasted_iota(jnp.int32, (HALF, 128), 0) + 2 * BLOCK * own_first
    degree = jnp.where(degree >= MW, degree - MW, degree)
    lane_n = lax.broadcasted_iota(jnp.int32, (HALF, 128), 1)
    for gp in range(6):
        gi, p = gp // 3, gp % 3
        first_slot = SLOTS * w + 16 * p + (z & 3) + 4 * gi
        m_a = mids_ref[first_slot]
        m_b = mids_ref[first_slot + 8] if p < 2 else m_a
        m = jnp.where(lane_n < PAIRS, m_a, m_b)
        parts = []
        for core in range(2):
            if p < 2:
                parts.append(recv_l[core, :, gi, BLOCK * p:BLOCK * p + BLOCK, :].astype(F32))
            else:
                packed = recv_l[core, :, gi, 2 * BLOCK:LEG_ROWS, :].astype(F32)
                swapped = jnp.concatenate([packed[:, :, 64:128], packed[:, :, 0:64]], axis=2)
                parts += [packed[:, 0:40], swapped[:, 0:40]]
        table = jnp.concatenate(parts, axis=1).reshape(HALF, 128)
        table = jnp.where(degree >= m, table, 0.0)
        rhs[gp, :, 0:128] = table.astype(BF16)
        rhs[gp, :, 128:256] = jnp.where(((degree + m) & 1) == 1, -table, table).astype(BF16)

    row_r = lax.broadcasted_iota(jnp.int32, (256, 128), 0) & 31
    j_r = row_r - GROUP * jnp.floor((row_r.astype(F32) + 0.5) * 0.2).astype(jnp.int32)
    slot_j[...] = j_r
    lane_r = lax.broadcasted_iota(jnp.int32, (32, 128), 1)
    pltpu.make_async_copy(recv_s, recv_s, ss_recv).wait()

    for gi in range(2):
        left = recv_s[:, 32 * gi:32 * gi + 32, :].reshape(256, HALF)
        terms = [jnp.dot(left, rhs[3 * gi + p], preferred_element_type=F32) for p in range(3)]
        j_r = slot_j[...]
        north, south = [
            jnp.where(j_r >= 4, terms[2][:, at:at + 128], jnp.where(j_r >= 2, terms[1][:, at:at + 128], terms[0][:, at:at + 128]))
            for at in (0, 128)
        ]
        odd = (j_r & 1) == 1
        north = jnp.where(odd, pltpu.roll(north, PAIRS, 1), north)
        south = jnp.where(odd, south, pltpu.roll(south, PAIRS, 1))
        both_halves = jnp.where(lane_r[0:1, :] < PAIRS, north, south)
        send_r[:, 32 * gi:32 * gi + 32, :] = both_halves.astype(BF16).reshape(CHIPS, 32, 128)

    def level_copy(k):
        to = lax.rem(z + k, CHIPS)
        return pltpu.make_async_remote_copy(
            src_ref=send_r.at[to], dst_ref=recv_x.at[z], send_sem=sx_send,
            recv_sem=sx_recv, device_id={"lev": 2 * to + c}, device_id_type=MESH,
        )

    for k in sorted(range(1, CHIPS), key=lambda k: abs(k - CHIPS // 2)):
        level_copy(k).start()
    pltpu.make_async_copy(send_r.at[z], recv_x.at[z], sx_recv).start()
    pltpu.make_async_copy(recv_x, recv_x, sx_recv).wait()

    got = recv_x[...].astype(F32)
    got = got[0:4] + got[4:8]
    level_sums = jnp.concatenate([got[:, 0:32], got[:, 32:64]], axis=0).reshape(256, 128).astype(BF16)
    by_slot = nt_dot(onehot[...], level_sums)
    low = by_slot[:, 0:128].reshape(WAVES, 8, 128)
    high = by_slot[:, 128:256].reshape(WAVES, 8, 128)
    send_y[...] = jnp.concatenate([low, high], axis=1).astype(BF16)

    def band_copy(dy, dx):
        to = 4 * ((w // 4 + dy) & 7) + ((w + dx) & 3)
        seat = 16 * (dy % 2) + 4 * (dy // 2) + dx
        return pltpu.make_async_remote_copy(
            src_ref=send_y.at[to], dst_ref=recv_z.at[seat], send_sem=sz_send,
            recv_sem=sz_recv.at[dy % 2], device_id={"wave": to}, device_id_type=MESH,
        )

    moves = [(dy, dx) for dy in (4, 2, 6, 0, 3, 5, 1, 7) for dx in (2, 1, 3, 0) if dy or dx]
    for dy, dx in moves:
        band_copy(dy, dx).start()
    pltpu.make_async_copy(send_y.at[w], recv_z.at[0], sz_recv.at[0]).start()

    for part in range(2):
        arrived = recv_z.at[pl.ds(16 * part, 16)]
        pltpu.make_async_copy(arrived, arrived, sz_recv.at[part]).wait()
        zf[...] = arrived[...].astype(F32).reshape(256, 128)
        for slot in range(LAT_MAX):
            zs[32 * slot:32 * slot + 32, :] = zf[pl.ds(slot, 32, stride=8), :].astype(BF16)
        for i in range(20):
            both = jnp.dot(zs[...], expand[i], preferred_element_type=F32)
            table_at = HALF * part + 32 * i
            at = MW * part + 32 * i
            for slot in range(LAT_MAX):
                re = both[32 * slot:32 * slot + 32, 0:128]
                im = both[32 * slot:32 * slot + 32, 128:256]
                cos_part = cosc[slot, table_at:table_at + 32, :]
                sin_part = sinc[slot, table_at:table_at + 32, :]
                mod[slot, at:at + 32, :] = (re * cos_part - im * sin_part).astype(BF16)
                mod[slot, at + HALF:at + HALF + 32, :] = (re * sin_part + im * cos_part).astype(BF16)
        for slot in range(LAT_MAX):
            points = jnp.dot(
                tw[slot, :, MW * part:MW * part + MW], mod[slot, MW * part:MW * part + MW, :],
                preferred_element_type=F32,
            )
            if part == 0:
                partial[slot] = points
            else:
                lat[pl.ds(slot, 128, stride=8), :] = (partial[slot] + points).T

    slot_of = lax.broadcasted_iota(jnp.int32, (8, 128), 0)
    lon = lax.broadcasted_iota(jnp.int32, (8, 128), 1)
    cycles = jnp.zeros((8, 128), jnp.int32)
    for slot in range(LAT_MAX):
        cycles = jnp.where(slot_of == slot, cycle_of(slot), cycles)
    for f in range(3):
        for kh in range(KH):
            at = 8 * (KH * f + kh)
            width = min(128, NLON_MAX - 128 * kh)
            tile = jnp.where(lon + 128 * kh < cycles, lat[at:at + 8, :], 0.0).astype(BF16)
            out_ref[f, :, 128 * kh:128 * kh + width] = tile[:, 0:width]

    def all_sent(block, count, sem):
        part = block.at[pl.ds(0, count)]
        pltpu.make_async_copy(part, part, sem).wait()

    all_sent(recv_s, CHIPS - 1, ss_send)
    all_sent(recv_l.at[0], 3, sl_send)
    all_sent(recv_l.at[0], 4, sf_send)
    all_sent(recv_x, CHIPS - 1, sx_send)
    all_sent(send_y, WAVES - 1, sz_send)


def on_device(spec, legendre, mids, band_lats, nlon):
    spec_rows = spec.reshape(240, MW)
    tables = jnp.transpose(legendre, (0, 2, 1))
    hbm = pl.BlockSpec(memory_space=pltpu.HBM)
    vmem = pl.BlockSpec(memory_space=pltpu.VMEM)
    dma = pltpu.SemaphoreType.DMA
    planes = pl.pallas_call(
        kernel,
        out_shape=jax.ShapeDtypeStruct((3, LAT_MAX, NLON_MAX), BF16),
        in_specs=[hbm] * 6,
        out_specs=vmem,
        scratch_shapes=[
            pltpu.SMEM((MW,), jnp.int32),
            pltpu.SMEM((WAVES,), jnp.int32),
            pltpu.SMEM((PAIRS,), jnp.int32),
            pltpu.VMEM((240, MW), BF16),
            pltpu.VMEM((SLOTS, PAIRS, BLOCK), BF16),
            pltpu.VMEM((16, 128), jnp.int32),
            pltpu.VMEM((1, MW), F32),
            pltpu.VMEM((10, 256, 128), F32),
            pltpu.VMEM((CHIPS, 64, HALF), BF16),
            pltpu.VMEM((4, 2, LEG_ROWS, 128), BF16),
            pltpu.VMEM((CHIPS, 64, HALF), BF16),
            pltpu.VMEM((2, 4, 2, LEG_ROWS, 128), BF16),
            pltpu.VMEM((6, HALF, 256), BF16),
            pltpu.VMEM((256, 128), jnp.int32),
            pltpu.VMEM((CHIPS, 64, 128), BF16),
            pltpu.VMEM((CHIPS, 64, 128), BF16),
            pltpu.VMEM((256, 128), BF16),
            pltpu.VMEM((WAVES, 16, 128), BF16),
            pltpu.VMEM((WAVES, 16, 128), BF16),
            pltpu.VMEM((256, 128), F32),
            pltpu.VMEM((256, 128), BF16),
            pltpu.VMEM((20, 128, 256), BF16),
            pltpu.VMEM((MW, 128), F32),
            pltpu.VMEM((LAT_MAX, MW, 128), F32),
            pltpu.VMEM((LAT_MAX, MW, 128), F32),
            pltpu.VMEM((LAT_MAX, 128, 2 * MW), BF16),
            pltpu.VMEM((LAT_MAX, 2 * MW, 128), BF16),
            pltpu.VMEM((LAT_MAX, 128, 128), F32),
            pltpu.VMEM((1024, 128), F32),
            dma((6,)), dma, dma, dma, dma((4,)), dma, dma, dma, dma, dma, dma((2,)),
        ],
        compiler_params=pltpu.CompilerParams(
            collective_id=0, has_side_effects=True, vmem_limit_bytes=58 * 2**20
        ),
    )(mids, band_lats, nlon, spec_rows, tables, mids.reshape(10, 128))
    return jnp.transpose(planes, (1, 0, 2)).reshape(LAT_MAX, 3, 1, NLON_MAX)


def solution(mesh):
    in_specs = (P(None, None, "lev", "wave", None), P("wave", "lev", None), P(), P(), P())
    out_specs = P("wave", None, "lev", None)
    return jax.shard_map(
        on_device, mesh=mesh, in_specs=in_specs, out_specs=out_specs, check_vma=False
    )
```

```python
import jax
import jax.numpy as jnp
from jax import lax
from jax.experimental import pallas as pl
from jax.experimental.pallas import tpu as pltpu
from jax.sharding import PartitionSpec as P

LAT_MAX = 8
NLON_MAX = 5136
KH = 41
WAVES = 32
LEVS = 16
CHIPS = 8
SLOTS = 40
GROUP = 5
HALF = 640
MW = 1280
BLOCK = 80
LEG_ROWS = 208
PAIRS = 64
LATS = 128
TWO_PI = 6.283185307179586
F32 = jnp.float32
BF16 = jnp.bfloat16
MESH = pl.DeviceIdType.MESH

SIN = []
_term = TWO_PI
for _i in range(6):
    SIN.append(_term)
    _term = -_term * TWO_PI * TWO_PI / ((2 * _i + 2) * (2 * _i + 3))


def quarter_sine(y):
    y2 = y * y
    acc = jnp.full_like(y2, SIN[-1])
    for c in SIN[-2::-1]:
        acc = acc * y2 + c
    return acc * y


def cos_sin(steps, cycle, inverse):
    rest = steps - jnp.floor(steps * inverse + 0.5) * cycle
    t = rest * inverse
    a = jnp.abs(t)
    folded = jnp.where(a > 0.25, jnp.where(t < 0, -0.5, 0.5) - t, t)
    return quarter_sine(0.25 - a), quarter_sine(folded)


def nt_dot(a, b):
    return lax.dot_general(a, b, (((1,), (1,)), ((), ())), preferred_element_type=F32)


def kernel(
    mids_hbm, bands_hbm, nlon_hbm, spec_hbm, leg_hbm, mids_rows_hbm, out_ref,
    mids_ref, bands_ref, nlon_ref, spec_ref, leg_ref, mids_rows, mrow_ref, spec_f, send_s, send_l, recv_s, recv_l, rhs, slot_j, send_r, recv_x,
    onehot, send_y, recv_z, zf, zs, expand, mcol, cosc, sinc, tw, mod, partial, lat,
    load_sem, ss_send, ss_recv, sl_send, sl_recv, sf_send, sf_recv, sx_send, sx_recv, sz_send, sz_recv,
):
    w = lax.axis_index("wave")
    me = lax.axis_index("lev")
    z = me // 2
    c = me - 2 * z

    mids_rows[...] = jnp.zeros_like(mids_rows)
    loads = [
        pltpu.make_async_copy(leg_hbm, leg_ref, load_sem.at[0]),
        pltpu.make_async_copy(spec_hbm, spec_ref, load_sem.at[1]),
        pltpu.make_async_copy(mids_rows_hbm, mids_rows.at[0:10], load_sem.at[2]),
        pltpu.make_async_copy(mids_hbm, mids_ref, load_sem.at[3]),
        pltpu.make_async_copy(bands_hbm, bands_ref, load_sem.at[4]),
        pltpu.make_async_copy(nlon_hbm, nlon_ref, load_sem.at[5]),
    ]
    for load in loads:
        load.start()

    barrier = pltpu.get_barrier_semaphore()
    for k in sorted(range(1, CHIPS), key=lambda k: abs(k - CHIPS // 2)):
        peer = 2 * lax.rem(z + k, CHIPS) + c
        pl.semaphore_signal(barrier, inc=1, device_id={"lev": peer}, device_id_type=MESH)
    sibling = 2 * z + (1 - c)
    pl.semaphore_signal(barrier, inc=1, device_id={"lev": sibling}, device_id_type=MESH)
    for k in range(1, WAVES):
        pl.semaphore_signal(barrier, inc=1, device_id={"wave": lax.rem(w + k, WAVES)}, device_id_type=MESH)


    unit = jnp.where(
        lax.broadcasted_iota(jnp.int32, (BLOCK, BLOCK), 0) == lax.broadcasted_iota(jnp.int32, (BLOCK, BLOCK), 1),
        1.0, 0.0,
    ).astype(BF16)

    fold = jnp.where(
        (lax.broadcasted_iota(jnp.int32, (48, BLOCK), 0) == lax.broadcasted_iota(jnp.int32, (48, BLOCK), 1))
        | (lax.broadcasted_iota(jnp.int32, (48, BLOCK), 0) + 40 == lax.broadcasted_iota(jnp.int32, (48, BLOCK), 1)),
        1.0, 0.0,
    )
    fold = jnp.where(lax.broadcasted_iota(jnp.int32, (48, BLOCK), 0) < 40, fold, 0.0).astype(BF16)
    upper = (lax.broadcasted_iota(jnp.int32, (LATS, BLOCK), 0) < PAIRS) == (
        lax.broadcasted_iota(jnp.int32, (LATS, BLOCK), 1) < 40
    )
    loads[0].wait()

    def first_chip(chip):
        return (chip + 6 + (chip & 1)) & 7

    own_first = first_chip(z)

    def spec_copy(k):
        to = lax.rem(z + k, CHIPS)
        return pltpu.make_async_remote_copy(
            src_ref=send_s.at[to], dst_ref=recv_s.at[z], send_sem=ss_send,
            recv_sem=ss_recv, device_id={"lev": 2 * to + c}, device_id_type=MESH,
        )

    def leg_copy(to):
        seat = (z - first_chip(to)) & 7
        return pltpu.make_async_remote_copy(
            src_ref=send_l.at[to & 3], dst_ref=recv_l.at[c, seat], send_sem=sl_send,
            recv_sem=sl_recv.at[seat], device_id={"lev": 2 * to + c}, device_id_type=MESH,
        )

    def share_copy(seat):
        return pltpu.make_async_remote_copy(
            src_ref=recv_l.at[c, seat], dst_ref=recv_l.at[c, seat], send_sem=sf_send,
            recv_sem=sf_recv, device_id={"lev": sibling}, device_id_type=MESH,
        )

    def order_of(i):
        return jnp.where(lax.rem(i, 2) == 1, 4 - (i + 1) // 2, 4 + i // 2)

    def prepare_leg(low, gi):
        group = low + 4 * gi
        for p in range(2):
            stacked = jnp.concatenate([leg_ref[16 * p + group], leg_ref[16 * p + 8 + group]], axis=0)
            send_l[low, gi, BLOCK * p:BLOCK * p + BLOCK, :] = nt_dot(unit, stacked).astype(BF16)
        last = leg_ref[32 + group].astype(F32)
        stacked = jnp.where(upper, jnp.concatenate([last, last], axis=0), 0.0).astype(BF16)
        send_l[low, gi, 2 * BLOCK:LEG_ROWS, :] = nt_dot(fold, stacked).astype(BF16)

    lane_s = lax.broadcasted_iota(jnp.int32, (32, 128), 1)

    def prepare_spec(k):
        to = lax.rem(z + k, CHIPS)
        start = 2 * BLOCK * first_chip(to)
        shift = start & 127
        for gi in range(2):
            turned = []
            for u in range(6):
                tile = lax.rem((start >> 7) + u, 10)
                rows = spec_f[tile, pl.ds((to & 3) + 4 * gi, 32, stride=8), :]
                turned.append(pltpu.roll(rows, (128 - shift) & 127, 1))
            for u in range(5):
                rows = jnp.where(lane_s < 128 - shift, turned[u], turned[u + 1])
                send_s[to, 32 * gi:32 * gi + 32, 128 * u:128 * u + 128] = rows.astype(BF16)

    for low in range(4):
        for gi in range(2):
            prepare_leg(low, gi)
    loads[1].wait()
    for tile in range(10):
        spec_f[tile, 0:240, :] = spec_ref[:, 128 * tile:128 * tile + 128].astype(F32)
        spec_f[tile, 240:256, :] = jnp.zeros((16, 128), F32)

    def prepare_all(k, carry):
        prepare_spec(k)
        return carry

    lax.fori_loop(0, CHIPS, prepare_all, 0)
    pl.semaphore_wait(barrier, CHIPS + WAVES - 1)
    for to in ((z + 2 - 4 * (z & 1)) & 7, (z + 1) & 7, (z + 7) & 7):
        leg_copy(to).start()
    own_seat = (z - own_first) & 7
    pltpu.make_async_copy(send_l.at[z & 3], recv_l.at[c, own_seat], sl_recv.at[own_seat]).start()

    def send_spec(i, carry):
        spec_copy(order_of(i)).start()
        return carry

    lax.fori_loop(0, CHIPS - 1, send_spec, 0, unroll=7)
    pltpu.make_async_copy(send_s.at[z], recv_s.at[z], ss_recv).start()

    for load in loads[2:]:
        load.wait()

    start = jnp.int32(0)
    own_start = jnp.int32(0)
    sub16 = lax.broadcasted_iota(jnp.int32, (16, 128), 0)
    lane = lax.broadcasted_iota(jnp.int32, (16, 128), 1)
    lat_of = jnp.where(lane < PAIRS, lane, LATS - 1 - (lane - PAIRS))
    for e in range(WAVES // 2):
        count_a, count_b = bands_ref[2 * e], bands_ref[2 * e + 1]
        start_b = start + count_a
        own_start = jnp.where(w == 2 * e, start, jnp.where(w == 2 * e + 1, start_b, own_start))
        inner = sub16 & 7
        wanted = jnp.where(sub16 < 8, start, start_b) + inner
        filled = inner < jnp.where(sub16 < 8, count_a, count_b)
        match = jnp.where(filled, wanted, -1) == lat_of
        onehot[16 * e:16 * e + 16, :] = jnp.where(match, 1.0, 0.0).astype(BF16)
        start = start_b + count_b

    def cycle_of(slot):
        latitude = jnp.minimum(own_start + slot, LATS - 1)
        pair = jnp.where(latitude < PAIRS, latitude, LATS - 1 - latitude)
        return nlon_ref[pair]

    krow = lax.broadcasted_iota(jnp.int32, (128, 256), 0)
    klane = lax.broadcasted_iota(jnp.int32, (128, 256), 1)
    col = klane & 127
    channel = jnp.where(col >= KH, 1, 0) + jnp.where(col >= 2 * KH, 1, 0) + jnp.where(col >= 3 * KH, 100, 0)
    base = krow - (GROUP * channel + jnp.where(klane >= 128, 15, 0))

    def fill_expand(i, carry):
        zl = i // GROUP
        match = base == zl * 32 + (i - GROUP * zl)
        expand[i] = jnp.where(match, 1.0, 0.0).astype(BF16)
        return carry

    lax.fori_loop(0, 20, fill_expand, 0)

    natural = mids_rows[...].astype(F32)
    high = jnp.floor(natural * 0.125)
    digits = jnp.concatenate([high, natural - 8.0 * high], axis=0).astype(BF16)
    for t in range(10):
        place = lax.broadcasted_iota(jnp.int32, (128, 128), 1) + 128 * t
        wave_half = jnp.where(place >= HALF, 1, 0)
        inner = place - HALF * wave_half
        group = inner >> 5
        zl = jnp.where(group >= 5, 1, 0) + jnp.where(group >= 10, 1, 0) + jnp.where(group >= 15, 1, 0)
        seat = (inner & 31) >> 1
        from_y = (w // 4 - (2 * (seat >> 2) + wave_half) + 8) & 7
        from_x = ((w & 3) - (seat & 3) + 4) & 3
        source = SLOTS * (4 * from_y + from_x) + 8 * (group - GROUP * zl) + 4 * (place & 1) + zl
        pick = lax.broadcasted_iota(jnp.int32, (128, 128), 0) == (source & 127)
        found = jnp.dot(digits, jnp.where(pick, 1.0, 0.0).astype(BF16), preferred_element_type=F32)
        found = 8.0 * found[0:16, :] + found[16:32, :]
        here = lax.broadcasted_iota(jnp.int32, (16, 128), 0) == (source[0:16, :] >> 7)
        row = jnp.sum(jnp.where(here, found, 0.0), axis=0, keepdims=True)
        mrow_ref[0:1, 128 * t:128 * t + 128] = row
        mcol[128 * t:128 * t + 128, :] = jnp.broadcast_to(row, (128, 128)).T

    col1 = lax.broadcasted_iota(jnp.int32, (1, 128), 1)
    channel1 = jnp.where(col1 >= KH, 1, 0) + jnp.where(col1 >= 2 * KH, 1, 0)
    coarse_steps = (128 * (col1 - KH * channel1)).astype(F32)
    a_steps = (16 * lax.broadcasted_iota(jnp.int32, (8, 128), 0)).astype(F32)
    b_steps = lax.broadcasted_iota(jnp.int32, (16, 128), 0).astype(F32)

    def tables(slot, carry):
        cycle = jnp.full((1, 128), cycle_of(slot), jnp.int32).astype(F32)
        inverse = 1.0 / cycle

        def coarse(i, inner_carry):
            at = pl.multiple_of(128 * i, 128)
            cos_part, sin_part = cos_sin(mcol[pl.ds(at, 128), :] * coarse_steps, cycle, inverse)
            cosc[slot, pl.ds(at, 128), :] = cos_part
            sinc[slot, pl.ds(at, 128), :] = sin_part
            return inner_carry

        lax.fori_loop(0, 10, coarse, 0)

        def fine(i, inner_carry):
            m = mrow_ref[0:1, pl.ds(pl.multiple_of(128 * i, 128), 128)]
            at = pl.multiple_of(128 * i + jnp.where(i >= 5, HALF, 0), 128)
            weight = jnp.where(m == 0, 1.0, 2.0)
            weight = jnp.where(2 * m < cycle, weight, 0.0)
            cos_a, sin_a = cos_sin(m * a_steps, cycle, inverse)
            cos_b, sin_b = cos_sin(m * b_steps, cycle, inverse)
            cos_a = cos_a * weight
            sin_a = sin_a * weight
            for a in range(8):
                ca, sa = cos_a[a:a + 1, :], sin_a[a:a + 1, :]
                tw[slot, 16 * a:16 * a + 16, pl.ds(at, 128)] = (ca * cos_b - sa * sin_b).astype(BF16)
                other = pl.multiple_of(at + HALF, 128)
                tw[slot, 16 * a:16 * a + 16, pl.ds(other, 128)] = (-(sa * cos_b + ca * sin_b)).astype(BF16)
            return inner_carry

        lax.fori_loop(0, 10, fine, 0)
        return carry

    lax.fori_loop(0, LAT_MAX, tables, 0)

    for seat in range(4):
        pltpu.make_async_copy(recv_l.at[c, seat], recv_l.at[c, seat], sl_recv.at[seat]).wait()
        share_copy(seat).start()
    pltpu.make_async_copy(recv_l.at[1 - c], recv_l.at[1 - c], sf_recv).wait()
    degree = lax.broadcasted_iota(jnp.int32, (HALF, 128), 0) + 2 * BLOCK * own_first
    degree = jnp.where(degree >= MW, degree - MW, degree)
    lane_n = lax.broadcasted_iota(jnp.int32, (HALF, 128), 1)
    for gp in range(6):
        gi, p = gp // 3, gp % 3
        first_slot = SLOTS * w + 16 * p + (z & 3) + 4 * gi
        m_a = mids_ref[first_slot]
        m_b = mids_ref[first_slot + 8] if p < 2 else m_a
        m = jnp.where(lane_n < PAIRS, m_a, m_b)
        parts = []
        for core in range(2):
            if p < 2:
                parts.append(recv_l[core, :, gi, BLOCK * p:BLOCK * p + BLOCK, :].astype(F32))
            else:
                packed = recv_l[core, :, gi, 2 * BLOCK:LEG_ROWS, :].astype(F32)
                swapped = jnp.concatenate([packed[:, :, 64:128], packed[:, :, 0:64]], axis=2)
                parts += [packed[:, 0:40], swapped[:, 0:40]]
        table = jnp.concatenate(parts, axis=1).reshape(HALF, 128)
        table = jnp.where(degree >= m, table, 0.0)
        rhs[gp, :, 0:128] = table.astype(BF16)
        rhs[gp, :, 128:256] = jnp.where(((degree + m) & 1) == 1, -table, table).astype(BF16)

    row_r = lax.broadcasted_iota(jnp.int32, (256, 128), 0) & 31
    j_r = row_r - GROUP * jnp.floor((row_r.astype(F32) + 0.5) * 0.2).astype(jnp.int32)
    slot_j[...] = j_r
    lane_r = lax.broadcasted_iota(jnp.int32, (32, 128), 1)
    pltpu.make_async_copy(recv_s, recv_s, ss_recv).wait()

    for gi in range(2):
        left = recv_s[:, 32 * gi:32 * gi + 32, :].reshape(256, HALF)
        terms = [jnp.dot(left, rhs[3 * gi + p], preferred_element_type=F32) for p in range(3)]
        j_r = slot_j[...]
        north, south = [
            jnp.where(j_r >= 4, terms[2][:, at:at + 128], jnp.where(j_r >= 2, terms[1][:, at:at + 128], terms[0][:, at:at + 128]))
            for at in (0, 128)
        ]
        odd = (j_r & 1) == 1
        north = jnp.where(odd, pltpu.roll(north, PAIRS, 1), north)
        south = jnp.where(odd, south, pltpu.roll(south, PAIRS, 1))
        both_halves = jnp.where(lane_r[0:1, :] < PAIRS, north, south)
        send_r[:, 32 * gi:32 * gi + 32, :] = both_halves.astype(BF16).reshape(CHIPS, 32, 128)

    def level_copy(k):
        to = lax.rem(z + k, CHIPS)
        return pltpu.make_async_remote_copy(
            src_ref=send_r.at[to], dst_ref=recv_x.at[z], send_sem=sx_send,
            recv_sem=sx_recv, device_id={"lev": 2 * to + c}, device_id_type=MESH,
        )

    for k in sorted(range(1, CHIPS), key=lambda k: abs(k - CHIPS // 2)):
        level_copy(k).start()
    pltpu.make_async_copy(send_r.at[z], recv_x.at[z], sx_recv).start()
    pltpu.make_async_copy(recv_x, recv_x, sx_recv).wait()

    got = recv_x[...].astype(F32)
    got = got[0:4] + got[4:8]
    level_sums = jnp.concatenate([got[:, 0:32], got[:, 32:64]], axis=0).reshape(256, 128).astype(BF16)
    by_slot = nt_dot(onehot[...], level_sums)
    low = by_slot[:, 0:128].reshape(WAVES, 8, 128)
    high = by_slot[:, 128:256].reshape(WAVES, 8, 128)
    send_y[...] = jnp.concatenate([low, high], axis=1).astype(BF16)

    def band_copy(dy, dx):
        to = 4 * ((w // 4 + dy) & 7) + ((w + dx) & 3)
        seat = 16 * (dy % 2) + 4 * (dy // 2) + dx
        return pltpu.make_async_remote_copy(
            src_ref=send_y.at[to], dst_ref=recv_z.at[seat], send_sem=sz_send,
            recv_sem=sz_recv.at[dy % 2], device_id={"wave": to}, device_id_type=MESH,
        )

    moves = [(dy, dx) for dy in (4, 2, 6, 0, 3, 5, 1, 7) for dx in (2, 1, 3, 0) if dy or dx]
    for dy, dx in moves:
        band_copy(dy, dx).start()
    pltpu.make_async_copy(send_y.at[w], recv_z.at[0], sz_recv.at[0]).start()

    for part in range(2):
        arrived = recv_z.at[pl.ds(16 * part, 16)]
        pltpu.make_async_copy(arrived, arrived, sz_recv.at[part]).wait()
        zf[...] = arrived[...].astype(F32).reshape(256, 128)
        for slot in range(LAT_MAX):
            zs[32 * slot:32 * slot + 32, :] = zf[pl.ds(slot, 32, stride=8), :].astype(BF16)
        for i in range(20):
            both = jnp.dot(zs[...], expand[i], preferred_element_type=F32)
            table_at = HALF * part + 32 * i
            at = MW * part + 32 * i
            for slot in range(LAT_MAX):
                re = both[32 * slot:32 * slot + 32, 0:128]
                im = both[32 * slot:32 * slot + 32, 128:256]
                cos_part = cosc[slot, table_at:table_at + 32, :]
                sin_part = sinc[slot, table_at:table_at + 32, :]
                mod[slot, at:at + 32, :] = (re * cos_part - im * sin_part).astype(BF16)
                mod[slot, at + HALF:at + HALF + 32, :] = (re * sin_part + im * cos_part).astype(BF16)
        for slot in range(LAT_MAX):
            points = jnp.dot(
                tw[slot, :, MW * part:MW * part + MW], mod[slot, MW * part:MW * part + MW, :],
                preferred_element_type=F32,
            )
            if part == 0:
                partial[slot] = points
            else:
                lat[pl.ds(slot, 128, stride=8), :] = (partial[slot] + points).T

    slot_of = lax.broadcasted_iota(jnp.int32, (8, 128), 0)
    lon = lax.broadcasted_iota(jnp.int32, (8, 128), 1)
    cycles = jnp.zeros((8, 128), jnp.int32)
    for slot in range(LAT_MAX):
        cycles = jnp.where(slot_of == slot, cycle_of(slot), cycles)
    for f in range(3):
        for kh in range(KH):
            at = 8 * (KH * f + kh)
            width = min(128, NLON_MAX - 128 * kh)
            tile = jnp.where(lon + 128 * kh < cycles, lat[at:at + 8, :], 0.0).astype(BF16)
            out_ref[f, :, 128 * kh:128 * kh + width] = tile[:, 0:width]

    def all_sent(block, count, sem):
        part = block.at[pl.ds(0, count)]
        pltpu.make_async_copy(part, part, sem).wait()

    all_sent(recv_s, CHIPS - 1, ss_send)
    all_sent(recv_l.at[0], 3, sl_send)
    all_sent(recv_l.at[0], 4, sf_send)
    all_sent(recv_x, CHIPS - 1, sx_send)
    all_sent(send_y, WAVES - 1, sz_send)


def on_device(spec, legendre, mids, band_lats, nlon):
    spec_rows = spec.reshape(240, MW)
    tables = jnp.transpose(legendre, (0, 2, 1))
    hbm = pl.BlockSpec(memory_space=pltpu.HBM)
    vmem = pl.BlockSpec(memory_space=pltpu.VMEM)
    dma = pltpu.SemaphoreType.DMA
    planes = pl.pallas_call(
        kernel,
        out_shape=jax.ShapeDtypeStruct((3, LAT_MAX, NLON_MAX), BF16),
        in_specs=[hbm] * 6,
        out_specs=vmem,
        scratch_shapes=[
            pltpu.SMEM((MW,), jnp.int32),
            pltpu.SMEM((WAVES,), jnp.int32),
            pltpu.SMEM((PAIRS,), jnp.int32),
            pltpu.VMEM((240, MW), BF16),
            pltpu.VMEM((SLOTS, PAIRS, BLOCK), BF16),
            pltpu.VMEM((16, 128), jnp.int32),
            pltpu.VMEM((1, MW), F32),
            pltpu.VMEM((10, 256, 128), F32),
            pltpu.VMEM((CHIPS, 64, HALF), BF16),
            pltpu.VMEM((4, 2, LEG_ROWS, 128), BF16),
            pltpu.VMEM((CHIPS, 64, HALF), BF16),
            pltpu.VMEM((2, 4, 2, LEG_ROWS, 128), BF16),
            pltpu.VMEM((6, HALF, 256), BF16),
            pltpu.VMEM((256, 128), jnp.int32),
            pltpu.VMEM((CHIPS, 64, 128), BF16),
            pltpu.VMEM((CHIPS, 64, 128), BF16),
            pltpu.VMEM((256, 128), BF16),
            pltpu.VMEM((WAVES, 16, 128), BF16),
            pltpu.VMEM((WAVES, 16, 128), BF16),
            pltpu.VMEM((256, 128), F32),
            pltpu.VMEM((256, 128), BF16),
            pltpu.VMEM((20, 128, 256), BF16),
            pltpu.VMEM((MW, 128), F32),
            pltpu.VMEM((LAT_MAX, MW, 128), F32),
            pltpu.VMEM((LAT_MAX, MW, 128), F32),
            pltpu.VMEM((LAT_MAX, 128, 2 * MW), BF16),
            pltpu.VMEM((LAT_MAX, 2 * MW, 128), BF16),
            pltpu.VMEM((LAT_MAX, 128, 128), F32),
            pltpu.VMEM((1024, 128), F32),
            dma((6,)), dma, dma, dma, dma((4,)), dma, dma, dma, dma, dma, dma((2,)),
        ],
        compiler_params=pltpu.CompilerParams(
            collective_id=0, has_side_effects=True, vmem_limit_bytes=58 * 2**20
        ),
    )(mids, band_lats, nlon, spec_rows, tables, mids.reshape(10, 128))
    return jnp.transpose(planes, (1, 0, 2)).reshape(LAT_MAX, 3, 1, NLON_MAX)


def solution(mesh):
    in_specs = (P(None, None, "lev", "wave", None), P("wave", "lev", None), P(), P(), P())
    out_specs = P("wave", None, "lev", None)
    return jax.shard_map(
        on_device, mesh=mesh, in_specs=in_specs, out_specs=out_specs, check_vma=False
    )
```

```python
import jax
import jax.numpy as jnp
from jax import lax
from jax.experimental import pallas as pl
from jax.experimental.pallas import tpu as pltpu
from jax.sharding import PartitionSpec as P

LAT_MAX = 8
NLON_MAX = 5136
KH = 41
WAVES = 32
LEVS = 16
CHIPS = 8
SLOTS = 40
GROUP = 5
HALF = 640
MW = 1280
BLOCK = 80
LEG_ROWS = 208
PAIRS = 64
LATS = 128
TWO_PI = 6.283185307179586
F32 = jnp.float32
BF16 = jnp.bfloat16
MESH = pl.DeviceIdType.MESH

SIN = []
_term = TWO_PI
for _i in range(6):
    SIN.append(_term)
    _term = -_term * TWO_PI * TWO_PI / ((2 * _i + 2) * (2 * _i + 3))


def quarter_sine(y):
    y2 = y * y
    acc = jnp.full_like(y2, SIN[-1])
    for c in SIN[-2::-1]:
        acc = acc * y2 + c
    return acc * y


def cos_sin(steps, cycle, inverse):
    rest = steps - jnp.floor(steps * inverse + 0.5) * cycle
    t = rest * inverse
    a = jnp.abs(t)
    folded = jnp.where(a > 0.25, jnp.where(t < 0, -0.5, 0.5) - t, t)
    return quarter_sine(0.25 - a), quarter_sine(folded)


def nt_dot(a, b):
    return lax.dot_general(a, b, (((1,), (1,)), ((), ())), preferred_element_type=F32)


def kernel(
    mids_hbm, bands_hbm, nlon_hbm, spec_hbm, leg_hbm, mids_rows_hbm, out_ref,
    mids_ref, bands_ref, nlon_ref, spec_ref, leg_ref, mids_rows, mrow_ref, spec_f, send_s, send_l, recv_s, recv_l, rhs, slot_j, send_r, recv_x,
    onehot, send_y, recv_z, zf, zs, expand, mcol, cosc, sinc, tw, mod, partial, lat,
    load_sem, ss_send, ss_recv, sl_send, sl_recv, sf_send, sf_recv, sx_send, sx_recv, sz_send, sz_recv,
):
    w = lax.axis_index("wave")
    me = lax.axis_index("lev")
    z = me // 2
    c = me - 2 * z

    mids_rows[...] = jnp.zeros_like(mids_rows)
    loads = [
        pltpu.make_async_copy(leg_hbm, leg_ref, load_sem.at[0]),
        pltpu.make_async_copy(spec_hbm, spec_ref, load_sem.at[1]),
        pltpu.make_async_copy(mids_rows_hbm, mids_rows.at[0:10], load_sem.at[2]),
        pltpu.make_async_copy(mids_hbm, mids_ref, load_sem.at[3]),
        pltpu.make_async_copy(bands_hbm, bands_ref, load_sem.at[4]),
        pltpu.make_async_copy(nlon_hbm, nlon_ref, load_sem.at[5]),
    ]
    for load in loads:
        load.start()

    barrier = pltpu.get_barrier_semaphore()
    for k in sorted(range(1, CHIPS), key=lambda k: abs(k - CHIPS // 2)):
        peer = 2 * lax.rem(z + k, CHIPS) + c
        pl.semaphore_signal(barrier, inc=1, device_id={"lev": peer}, device_id_type=MESH)
    sibling = 2 * z + (1 - c)
    pl.semaphore_signal(barrier, inc=1, device_id={"lev": sibling}, device_id_type=MESH)
    for k in range(1, WAVES):
        pl.semaphore_signal(barrier, inc=1, device_id={"wave": lax.rem(w + k, WAVES)}, device_id_type=MESH)


    unit = jnp.where(
        lax.broadcasted_iota(jnp.int32, (BLOCK, BLOCK), 0) == lax.broadcasted_iota(jnp.int32, (BLOCK, BLOCK), 1),
        1.0, 0.0,
    ).astype(BF16)

    fold = jnp.where(
        (lax.broadcasted_iota(jnp.int32, (48, BLOCK), 0) == lax.broadcasted_iota(jnp.int32, (48, BLOCK), 1))
        | (lax.broadcasted_iota(jnp.int32, (48, BLOCK), 0) + 40 == lax.broadcasted_iota(jnp.int32, (48, BLOCK), 1)),
        1.0, 0.0,
    )
    fold = jnp.where(lax.broadcasted_iota(jnp.int32, (48, BLOCK), 0) < 40, fold, 0.0).astype(BF16)
    upper = (lax.broadcasted_iota(jnp.int32, (LATS, BLOCK), 0) < PAIRS) == (
        lax.broadcasted_iota(jnp.int32, (LATS, BLOCK), 1) < 40
    )
    loads[0].wait()

    def first_chip(chip):
        return (chip + 6 + (chip & 1)) & 7

    own_first = first_chip(z)

    def spec_copy(k):
        to = lax.rem(z + k, CHIPS)
        return pltpu.make_async_remote_copy(
            src_ref=send_s.at[to], dst_ref=recv_s.at[z], send_sem=ss_send,
            recv_sem=ss_recv, device_id={"lev": 2 * to + c}, device_id_type=MESH,
        )

    def leg_copy(to):
        seat = (z - first_chip(to)) & 7
        return pltpu.make_async_remote_copy(
            src_ref=send_l.at[to & 3], dst_ref=recv_l.at[c, seat], send_sem=sl_send,
            recv_sem=sl_recv.at[seat], device_id={"lev": 2 * to + c}, device_id_type=MESH,
        )

    def share_copy(seat):
        return pltpu.make_async_remote_copy(
            src_ref=recv_l.at[c, seat], dst_ref=recv_l.at[c, seat], send_sem=sf_send,
            recv_sem=sf_recv, device_id={"lev": sibling}, device_id_type=MESH,
        )

    def order_of(i):
        return jnp.where(lax.rem(i, 2) == 1, 4 - (i + 1) // 2, 4 + i // 2)

    def prepare_leg(low, gi):
        group = low + 4 * gi
        for p in range(2):
            stacked = jnp.concatenate([leg_ref[16 * p + group], leg_ref[16 * p + 8 + group]], axis=0)
            send_l[low, gi, BLOCK * p:BLOCK * p + BLOCK, :] = nt_dot(unit, stacked).astype(BF16)
        last = leg_ref[32 + group].astype(F32)
        stacked = jnp.where(upper, jnp.concatenate([last, last], axis=0), 0.0).astype(BF16)
        send_l[low, gi, 2 * BLOCK:LEG_ROWS, :] = nt_dot(fold, stacked).astype(BF16)

    lane_s = lax.broadcasted_iota(jnp.int32, (32, 128), 1)

    def prepare_spec(k):
        to = lax.rem(z + k, CHIPS)
        start = 2 * BLOCK * first_chip(to)
        shift = start & 127
        for gi in range(2):
            turned = []
            for u in range(6):
                tile = lax.rem((start >> 7) + u, 10)
                rows = spec_f[tile, pl.ds((to & 3) + 4 * gi, 32, stride=8), :]
                turned.append(pltpu.roll(rows, (128 - shift) & 127, 1))
            for u in range(5):
                rows = jnp.where(lane_s < 128 - shift, turned[u], turned[u + 1])
                send_s[to, 32 * gi:32 * gi + 32, 128 * u:128 * u + 128] = rows.astype(BF16)

    for low in range(4):
        for gi in range(2):
            prepare_leg(low, gi)
    loads[1].wait()
    for tile in range(10):
        spec_f[tile, 0:240, :] = spec_ref[:, 128 * tile:128 * tile + 128].astype(F32)
        spec_f[tile, 240:256, :] = jnp.zeros((16, 128), F32)

    def prepare_all(k, carry):
        prepare_spec(k)
        return carry

    lax.fori_loop(0, CHIPS, prepare_all, 0)
    pl.semaphore_wait(barrier, CHIPS + WAVES - 1)
    for to in ((z + 2 - 4 * (z & 1)) & 7, (z + 1) & 7, (z + 7) & 7):
        leg_copy(to).start()
    own_seat = (z - own_first) & 7
    pltpu.make_async_copy(send_l.at[z & 3], recv_l.at[c, own_seat], sl_recv.at[own_seat]).start()

    def send_spec(i, carry):
        spec_copy(order_of(i)).start()
        return carry

    lax.fori_loop(0, CHIPS - 1, send_spec, 0, unroll=7)
    pltpu.make_async_copy(send_s.at[z], recv_s.at[z], ss_recv).start()

    for load in loads[2:]:
        load.wait()

    start = jnp.int32(0)
    own_start = jnp.int32(0)
    sub16 = lax.broadcasted_iota(jnp.int32, (16, 128), 0)
    lane = lax.broadcasted_iota(jnp.int32, (16, 128), 1)
    lat_of = jnp.where(lane < PAIRS, lane, LATS - 1 - (lane - PAIRS))
    for e in range(WAVES // 2):
        count_a, count_b = bands_ref[2 * e], bands_ref[2 * e + 1]
        start_b = start + count_a
        own_start = jnp.where(w == 2 * e, start, jnp.where(w == 2 * e + 1, start_b, own_start))
        inner = sub16 & 7
        wanted = jnp.where(sub16 < 8, start, start_b) + inner
        filled = inner < jnp.where(sub16 < 8, count_a, count_b)
        match = jnp.where(filled, wanted, -1) == lat_of
        onehot[16 * e:16 * e + 16, :] = jnp.where(match, 1.0, 0.0).astype(BF16)
        start = start_b + count_b

    def cycle_of(slot):
        latitude = jnp.minimum(own_start + slot, LATS - 1)
        pair = jnp.where(latitude < PAIRS, latitude, LATS - 1 - latitude)
        return nlon_ref[pair]

    krow = lax.broadcasted_iota(jnp.int32, (128, 256), 0)
    klane = lax.broadcasted_iota(jnp.int32, (128, 256), 1)
    col = klane & 127
    channel = jnp.where(col >= KH, 1, 0) + jnp.where(col >= 2 * KH, 1, 0) + jnp.where(col >= 3 * KH, 100, 0)
    base = krow - (GROUP * channel + jnp.where(klane >= 128, 15, 0))

    def fill_expand(i, carry):
        zl = i // GROUP
        match = base == zl * 32 + (i - GROUP * zl)
        expand[i] = jnp.where(match, 1.0, 0.0).astype(BF16)
        return carry

    lax.fori_loop(0, 20, fill_expand, 0)

    natural = mids_rows[...].astype(F32)
    high = jnp.floor(natural * 0.125)
    digits = jnp.concatenate([high, natural - 8.0 * high], axis=0).astype(BF16)
    for t in range(10):
        place = lax.broadcasted_iota(jnp.int32, (128, 128), 1) + 128 * t
        wave_half = jnp.where(place >= HALF, 1, 0)
        inner = place - HALF * wave_half
        group = inner >> 5
        zl = jnp.where(group >= 5, 1, 0) + jnp.where(group >= 10, 1, 0) + jnp.where(group >= 15, 1, 0)
        seat = (inner & 31) >> 1
        from_y = (w // 4 - (2 * (seat >> 2) + wave_half) + 8) & 7
        from_x = ((w & 3) - (seat & 3) + 4) & 3
        source = SLOTS * (4 * from_y + from_x) + 8 * (group - GROUP * zl) + 4 * (place & 1) + zl
        pick = lax.broadcasted_iota(jnp.int32, (128, 128), 0) == (source & 127)
        found = jnp.dot(digits, jnp.where(pick, 1.0, 0.0).astype(BF16), preferred_element_type=F32)
        found = 8.0 * found[0:16, :] + found[16:32, :]
        here = lax.broadcasted_iota(jnp.int32, (16, 128), 0) == (source[0:16, :] >> 7)
        row = jnp.sum(jnp.where(here, found, 0.0), axis=0, keepdims=True)
        mrow_ref[0:1, 128 * t:128 * t + 128] = row
        mcol[128 * t:128 * t + 128, :] = jnp.broadcast_to(row, (128, 128)).T

    col1 = lax.broadcasted_iota(jnp.int32, (1, 128), 1)
    channel1 = jnp.where(col1 >= KH, 1, 0) + jnp.where(col1 >= 2 * KH, 1, 0)
    coarse_steps = (128 * (col1 - KH * channel1)).astype(F32)
    a_steps = (16 * lax.broadcasted_iota(jnp.int32, (8, 128), 0)).astype(F32)
    b_steps = lax.broadcasted_iota(jnp.int32, (16, 128), 0).astype(F32)

    def tables(slot, carry):
        cycle = jnp.full((1, 128), cycle_of(slot), jnp.int32).astype(F32)
        inverse = 1.0 / cycle

        def coarse(i, inner_carry):
            at = pl.multiple_of(128 * i, 128)
            cos_part, sin_part = cos_sin(mcol[pl.ds(at, 128), :] * coarse_steps, cycle, inverse)
            cosc[slot, pl.ds(at, 128), :] = cos_part
            sinc[slot, pl.ds(at, 128), :] = sin_part
            return inner_carry

        lax.fori_loop(0, 10, coarse, 0)

        def fine(i, inner_carry):
            m = mrow_ref[0:1, pl.ds(pl.multiple_of(128 * i, 128), 128)]
            at = pl.multiple_of(128 * i + jnp.where(i >= 5, HALF, 0), 128)
            weight = jnp.where(m == 0, 1.0, 2.0)
            weight = jnp.where(2 * m < cycle, weight, 0.0)
            cos_a, sin_a = cos_sin(m * a_steps, cycle, inverse)
            cos_b, sin_b = cos_sin(m * b_steps, cycle, inverse)
            cos_a = cos_a * weight
            sin_a = sin_a * weight
            for a in range(8):
                ca, sa = cos_a[a:a + 1, :], sin_a[a:a + 1, :]
                tw[slot, 16 * a:16 * a + 16, pl.ds(at, 128)] = (ca * cos_b - sa * sin_b).astype(BF16)
                other = pl.multiple_of(at + HALF, 128)
                tw[slot, 16 * a:16 * a + 16, pl.ds(other, 128)] = (-(sa * cos_b + ca * sin_b)).astype(BF16)
            return inner_carry

        lax.fori_loop(0, 10, fine, 0)
        return carry

    lax.fori_loop(0, LAT_MAX, tables, 0)

    for seat in range(4):
        pltpu.make_async_copy(recv_l.at[c, seat], recv_l.at[c, seat], sl_recv.at[seat]).wait()
        share_copy(seat).start()
    pltpu.make_async_copy(recv_l.at[1 - c], recv_l.at[1 - c], sf_recv).wait()
    degree = lax.broadcasted_iota(jnp.int32, (HALF, 128), 0) + 2 * BLOCK * own_first
    degree = jnp.where(degree >= MW, degree - MW, degree)
    lane_n = lax.broadcasted_iota(jnp.int32, (HALF, 128), 1)
    for gp in range(6):
        gi, p = gp // 3, gp % 3
        first_slot = SLOTS * w + 16 * p + (z & 3) + 4 * gi
        m_a = mids_ref[first_slot]
        m_b = mids_ref[first_slot + 8] if p < 2 else m_a
        m = jnp.where(lane_n < PAIRS, m_a, m_b)
        parts = []
        for core in range(2):
            if p < 2:
                parts.append(recv_l[core, :, gi, BLOCK * p:BLOCK * p + BLOCK, :].astype(F32))
            else:
                packed = recv_l[core, :, gi, 2 * BLOCK:LEG_ROWS, :].astype(F32)
                swapped = jnp.concatenate([packed[:, :, 64:128], packed[:, :, 0:64]], axis=2)
                parts += [packed[:, 0:40], swapped[:, 0:40]]
        table = jnp.concatenate(parts, axis=1).reshape(HALF, 128)
        table = jnp.where(degree >= m, table, 0.0)
        rhs[gp, :, 0:128] = table.astype(BF16)
        rhs[gp, :, 128:256] = jnp.where(((degree + m) & 1) == 1, -table, table).astype(BF16)

    row_r = lax.broadcasted_iota(jnp.int32, (256, 128), 0) & 31
    j_r = row_r - GROUP * jnp.floor((row_r.astype(F32) + 0.5) * 0.2).astype(jnp.int32)
    slot_j[...] = j_r
    lane_r = lax.broadcasted_iota(jnp.int32, (32, 128), 1)
    pltpu.make_async_copy(recv_s, recv_s, ss_recv).wait()

    for gi in range(2):
        left = recv_s[:, 32 * gi:32 * gi + 32, :].reshape(256, HALF)
        terms = [jnp.dot(left, rhs[3 * gi + p], preferred_element_type=F32) for p in range(3)]
        j_r = slot_j[...]
        north, south = [
            jnp.where(j_r >= 4, terms[2][:, at:at + 128], jnp.where(j_r >= 2, terms[1][:, at:at + 128], terms[0][:, at:at + 128]))
            for at in (0, 128)
        ]
        odd = (j_r & 1) == 1
        north = jnp.where(odd, pltpu.roll(north, PAIRS, 1), north)
        south = jnp.where(odd, south, pltpu.roll(south, PAIRS, 1))
        both_halves = jnp.where(lane_r[0:1, :] < PAIRS, north, south)
        send_r[:, 32 * gi:32 * gi + 32, :] = both_halves.astype(BF16).reshape(CHIPS, 32, 128)

    def level_copy(k):
        to = lax.rem(z + k, CHIPS)
        return pltpu.make_async_remote_copy(
            src_ref=send_r.at[to], dst_ref=recv_x.at[z], send_sem=sx_send,
            recv_sem=sx_recv, device_id={"lev": 2 * to + c}, device_id_type=MESH,
        )

    for k in sorted(range(1, CHIPS), key=lambda k: abs(k - CHIPS // 2)):
        level_copy(k).start()
    pltpu.make_async_copy(send_r.at[z], recv_x.at[z], sx_recv).start()
    pltpu.make_async_copy(recv_x, recv_x, sx_recv).wait()

    got = recv_x[...].astype(F32)
    got = got[0:4] + got[4:8]
    level_sums = jnp.concatenate([got[:, 0:32], got[:, 32:64]], axis=0).reshape(256, 128).astype(BF16)
    by_slot = nt_dot(onehot[...], level_sums)
    low = by_slot[:, 0:128].reshape(WAVES, 8, 128)
    high = by_slot[:, 128:256].reshape(WAVES, 8, 128)
    send_y[...] = jnp.concatenate([low, high], axis=1).astype(BF16)

    def band_copy(dy, dx):
        to = 4 * ((w // 4 + dy) & 7) + ((w + dx) & 3)
        seat = 16 * (dy % 2) + 4 * (dy // 2) + dx
        return pltpu.make_async_remote_copy(
            src_ref=send_y.at[to], dst_ref=recv_z.at[seat], send_sem=sz_send,
            recv_sem=sz_recv.at[dy % 2], device_id={"wave": to}, device_id_type=MESH,
        )

    moves = [(dy, dx) for dy in (3, 5, 1, 7, 4, 2, 6, 0) for dx in (2, 1, 3, 0) if dy or dx]
    for dy, dx in moves:
        band_copy(dy, dx).start()
    pltpu.make_async_copy(send_y.at[w], recv_z.at[0], sz_recv.at[0]).start()

    for part in (1, 0):
        arrived = recv_z.at[pl.ds(16 * part, 16)]
        pltpu.make_async_copy(arrived, arrived, sz_recv.at[part]).wait()
        zf[...] = arrived[...].astype(F32).reshape(256, 128)
        for slot in range(LAT_MAX):
            zs[32 * slot:32 * slot + 32, :] = zf[pl.ds(slot, 32, stride=8), :].astype(BF16)
        for i in range(20):
            both = jnp.dot(zs[...], expand[i], preferred_element_type=F32)
            table_at = HALF * part + 32 * i
            at = MW * part + 32 * i
            for slot in range(LAT_MAX):
                re = both[32 * slot:32 * slot + 32, 0:128]
                im = both[32 * slot:32 * slot + 32, 128:256]
                cos_part = cosc[slot, table_at:table_at + 32, :]
                sin_part = sinc[slot, table_at:table_at + 32, :]
                mod[slot, at:at + 32, :] = (re * cos_part - im * sin_part).astype(BF16)
                mod[slot, at + HALF:at + HALF + 32, :] = (re * sin_part + im * cos_part).astype(BF16)
        for slot in range(LAT_MAX):
            points = jnp.dot(
                tw[slot, :, MW * part:MW * part + MW], mod[slot, MW * part:MW * part + MW, :],
                preferred_element_type=F32,
            )
            if part == 1:
                partial[slot] = points
            else:
                lat[pl.ds(slot, 128, stride=8), :] = (partial[slot] + points).T

    slot_of = lax.broadcasted_iota(jnp.int32, (8, 128), 0)
    lon = lax.broadcasted_iota(jnp.int32, (8, 128), 1)
    cycles = jnp.zeros((8, 128), jnp.int32)
    for slot in range(LAT_MAX):
        cycles = jnp.where(slot_of == slot, cycle_of(slot), cycles)
    for f in range(3):
        for kh in range(KH):
            at = 8 * (KH * f + kh)
            width = min(128, NLON_MAX - 128 * kh)
            tile = jnp.where(lon + 128 * kh < cycles, lat[at:at + 8, :], 0.0).astype(BF16)
            out_ref[f, :, 128 * kh:128 * kh + width] = tile[:, 0:width]

    def all_sent(block, count, sem):
        part = block.at[pl.ds(0, count)]
        pltpu.make_async_copy(part, part, sem).wait()

    all_sent(recv_s, CHIPS - 1, ss_send)
    all_sent(recv_l.at[0], 3, sl_send)
    all_sent(recv_l.at[0], 4, sf_send)
    all_sent(recv_x, CHIPS - 1, sx_send)
    all_sent(send_y, WAVES - 1, sz_send)


def on_device(spec, legendre, mids, band_lats, nlon):
    spec_rows = spec.reshape(240, MW)
    tables = jnp.transpose(legendre, (0, 2, 1))
    hbm = pl.BlockSpec(memory_space=pltpu.HBM)
    vmem = pl.BlockSpec(memory_space=pltpu.VMEM)
    dma = pltpu.SemaphoreType.DMA
    planes = pl.pallas_call(
        kernel,
        out_shape=jax.ShapeDtypeStruct((3, LAT_MAX, NLON_MAX), BF16),
        in_specs=[hbm] * 6,
        out_specs=vmem,
        scratch_shapes=[
            pltpu.SMEM((MW,), jnp.int32),
            pltpu.SMEM((WAVES,), jnp.int32),
            pltpu.SMEM((PAIRS,), jnp.int32),
            pltpu.VMEM((240, MW), BF16),
            pltpu.VMEM((SLOTS, PAIRS, BLOCK), BF16),
            pltpu.VMEM((16, 128), jnp.int32),
            pltpu.VMEM((1, MW), F32),
            pltpu.VMEM((10, 256, 128), F32),
            pltpu.VMEM((CHIPS, 64, HALF), BF16),
            pltpu.VMEM((4, 2, LEG_ROWS, 128), BF16),
            pltpu.VMEM((CHIPS, 64, HALF), BF16),
            pltpu.VMEM((2, 4, 2, LEG_ROWS, 128), BF16),
            pltpu.VMEM((6, HALF, 256), BF16),
            pltpu.VMEM((256, 128), jnp.int32),
            pltpu.VMEM((CHIPS, 64, 128), BF16),
            pltpu.VMEM((CHIPS, 64, 128), BF16),
            pltpu.VMEM((256, 128), BF16),
            pltpu.VMEM((WAVES, 16, 128), BF16),
            pltpu.VMEM((WAVES, 16, 128), BF16),
            pltpu.VMEM((256, 128), F32),
            pltpu.VMEM((256, 128), BF16),
            pltpu.VMEM((20, 128, 256), BF16),
            pltpu.VMEM((MW, 128), F32),
            pltpu.VMEM((LAT_MAX, MW, 128), F32),
            pltpu.VMEM((LAT_MAX, MW, 128), F32),
            pltpu.VMEM((LAT_MAX, 128, 2 * MW), BF16),
            pltpu.VMEM((LAT_MAX, 2 * MW, 128), BF16),
            pltpu.VMEM((LAT_MAX, 128, 128), F32),
            pltpu.VMEM((1024, 128), F32),
            dma((6,)), dma, dma, dma, dma((4,)), dma, dma, dma, dma, dma, dma((2,)),
        ],
        compiler_params=pltpu.CompilerParams(
            collective_id=0, has_side_effects=True, vmem_limit_bytes=56098816
        ),
    )(mids, band_lats, nlon, spec_rows, tables, mids.reshape(10, 128))
    return jnp.transpose(planes, (1, 0, 2)).reshape(LAT_MAX, 3, 1, NLON_MAX)


def solution(mesh):
    in_specs = (P(None, None, "lev", "wave", None), P("wave", "lev", None), P(), P(), P())
    out_specs = P("wave", None, "lev", None)
    return jax.shard_map(
        on_device, mesh=mesh, in_specs=in_specs, out_specs=out_specs, check_vma=False
    )
```
